768 devices in a mesh: row: 12 (over z_lo, core), col: 64 (over x, z_hi, y).
Axes of the slice: x: 4, y: 8, z: 12 (z_hi: 2, z_lo: 6; z = z_hi * 6 + z_lo), core: 2. Of those that a mesh axis runs over, the one named last changes fastest.
Arguments:
- tiles: bfloat16 [12, 64, 64, 64, 128], P('row', 'col'), may hold values from -6 to 6
- dest_col: int32 [12, 64, 64, 1], P('row', 'col'), may hold values from 0 to 63, as said below
- mu_block: int32 [12, 64, 64], P('row', 'col'), may hold values from 0 to 31, as said below
- col_block: int32 [12, 64, 64], P('row', 'col'), may hold values from 0 to 3, as said below
- coeff: bfloat16 [24576, 1536], P('row', 'col'), may hold values from -0.0390625 to 0.0390625
Outputs:
- contracted: bfloat16 [1536, 32768], P('row', 'col')
The draws below stay inside these ranges and needn't reach their ends.
Inputs may be any that keep to these rules, and one draw needn't show every extreme that they name: `dest_col`: among the 64 blocks of one device at most 2 name the same column device, and in every draw some device sends exactly 2 to one column device. Every column device receives exactly 64 blocks from the devices of its row group. Blocks of one row group that name the same column device have distinct pairs (mu_block, col_block). `col_block`: see mu_block.
All inputs are finite; a program needn't handle non-finite values.
Results may differ from the reference program's by a relative error of at most 0.001.
Values may be sent and summed in bfloat16 or wider, within the bound.
No kernel may reach another device: no remote copies, remote signals or barrier semaphores. Data moves between devices by JAX's collectives and lax.ppermute only.
A program may use at most 32 MiB of HBM per device.

```python
import jax
import jax.numpy as jnp
from jax import lax

BLOCK = 64
COLW = 128
MB_DEV = 32
CB = 4
TILES = 64
CAP = 2
NMU = 24576
OCC = 1536
N_ROW = 12
N_COL = 64


def shared_layout(key):

    def pick_cells(cell_key):
        return jax.random.permutation(cell_key, MB_DEV * CB)

    def one_group(group_index):
        group_key = jax.random.fold_in(key, group_index)
        key_values, key_order, key_cells = jax.random.split(group_key, 3)
        scores = jax.random.permutation(key_values, N_COL).astype(jnp.int32)
        values = jnp.arange(N_COL)
        forced = jnp.where(values == N_COL // 2, -1, jnp.where(values == 1, -2, scores))
        scores = jnp.where(group_index == 0, forced, scores)
        shifts = jnp.argsort(scores).astype(jnp.int32)
        order = jax.random.permutation(key_order, TILES)
        offsets = shifts[order // CAP]
        senders = jnp.arange(N_COL)
        target = (senders[:, None] + offsets[None, :]) % N_COL
        cell_keys = jax.random.split(key_cells, N_COL)
        cell_table = jax.vmap(pick_cells)(cell_keys)[:, :TILES]
        cells = cell_table[target, jnp.arange(TILES)[None, :]]
        return (target, cells)
    return jax.vmap(one_group)(jnp.arange(N_ROW))


def draw_dest_col(key, part):
    target, cells = shared_layout(key)
    return target[..., None].astype(jnp.int32)


def draw_mu_block(key, part):
    target, cells = shared_layout(key)
    return (cells // CB).astype(jnp.int32)


def draw_col_block(key, part):
    target, cells = shared_layout(key)
    return (cells % CB).astype(jnp.int32)


def level_of(own_key, shape, pieces, least, top_value):
    loudness, own = 1.0, jax.random.fold_in(own_key, 6)
    for position, parts in pieces:
        heights = jnp.exp(jax.random.uniform(jax.random.fold_in(own, position), (parts,), jnp.float32, least / len(pieces), top_value / len(pieces)))
        loudness = loudness * jnp.repeat(heights, shape[position] // parts).reshape([-1 if axis == position else 1 for axis in range(len(shape))])
    return loudness


def normal_values(rng, dims, spread, bound, cuts=(), kind=jnp.bfloat16):
    factor_of = level_of(rng, dims, cuts, -0.22, 0.18) if cuts else 1.0
    entries = jax.random.normal(rng, dims, jnp.float32) * spread * factor_of
    return jnp.minimum(jnp.maximum(entries, -bound), bound).astype(kind)


def setup_inputs(seed: int = 0) -> dict:
    keys = jax.random.split(jax.random.key(seed), 6)
    return {
        "tiles": normal_values(keys[0], (N_ROW, N_COL, TILES, BLOCK, COLW), 1.0, 6.0, ((0, 12), (1, 64))),
        "dest_col": draw_dest_col(jax.random.fold_in(keys[5], 71), 0),
        "mu_block": draw_mu_block(jax.random.fold_in(keys[5], 71), 0),
        "col_block": draw_col_block(jax.random.fold_in(keys[5], 71), 0),
        "coeff": normal_values(keys[4], (NMU, OCC), NMU ** -0.5, 0.0390625, ((0, 12), (1, 64))),
    }


def reference(tiles, dest_col, mu_block, col_block, coeff):
    def add_group(group_index, running):
        tile_rows = tiles[group_index].reshape(N_COL * TILES, BLOCK, COLW).astype(jnp.float32)
        mu_index = mu_block[group_index].reshape(N_COL * TILES).astype(jnp.int32)
        column_index = (dest_col[group_index].reshape(N_COL * TILES) * CB + col_block[group_index].reshape(N_COL * TILES)).astype(jnp.int32)
        dense_tensor = jnp.zeros((MB_DEV, BLOCK, N_COL * CB, COLW), jnp.float32)
        dense_tensor = dense_tensor.at[mu_index, :, column_index, :].add(tile_rows)
        dense_tensor = dense_tensor.reshape(MB_DEV * BLOCK, N_COL * CB * COLW).astype(jnp.bfloat16)
        first_row = (group_index * MB_DEV * BLOCK).astype(jnp.int32)
        panel_rows = lax.dynamic_slice_in_dim(coeff, first_row, MB_DEV * BLOCK, 0)
        product = lax.dot_general(panel_rows, dense_tensor, (((0,), (0,)), ((), ())), preferred_element_type=jnp.float32)
        return running + product

    running = jnp.zeros((OCC, N_COL * CB * COLW), jnp.float32)
    running = lax.fori_loop(0, N_ROW, add_group, running)
    return running.astype(jnp.bfloat16)
```

```python
import functools

import jax
import jax.numpy as jnp
from jax import lax
from jax.experimental import pallas as pl
from jax.experimental.pallas import tpu as pltpu
from jax.sharding import PartitionSpec as P

CB = 4
CAP = 2
NX, NZH, NY = 4, 2, 8
NZL, NCORE = 6, 2
LABEL_ROWS = 16


def device(zl, core, x, zh, y):
    return (((zl * NCORE + core) * NX + x) * NZH + zh) * NY + y


def plane_groups():
    return [
        [device(zl, core, x, zh, y) for x in range(NX) for y in range(NY)]
        for zl in range(NZL)
        for core in range(NCORE)
        for zh in range(NZH)
    ]


def column_groups():
    return [
        [
            device(zl, core, x, zh, y)
            for zh in range(NZH)
            for zl in range(NZL)
            for core in range(NCORE)
        ]
        for x in range(NX)
        for y in range(NY)
    ]


def pack_kernel(dest, mu, colb, tiles, out, count):
    held, rows, cols = tiles.shape
    label_at = NZH * CAP * rows

    @pl.loop(0, NX * NZH * NY)
    def _(c):
        count[c] = 0

    @pl.loop(0, NX * NY)
    def _(j):
        out[j, pl.ds(label_at, LABEL_ROWS), :] = jnp.zeros((LABEL_ROWS, cols), out.dtype)

    lane = lax.broadcasted_iota(jnp.int32, (LABEL_ROWS, cols), 1)

    @pl.loop(0, held)
    def _(t):
        c = dest[t]
        rank = count[c]
        count[c] = rank + 1
        j = (c // (NZH * NY)) * NY + c % NY
        slot = ((c // NY) % NZH) * CAP + rank
        out[j, pl.ds(pl.multiple_of(slot * rows, rows), rows), :] = tiles[t]
        label = (mu[t] * CB + colb[t] + 1).astype(jnp.float32)
        old = out[j, pl.ds(label_at, LABEL_ROWS), :].astype(jnp.float32)
        out[j, pl.ds(label_at, LABEL_ROWS), :] = jnp.where(lane == slot, label, old).astype(out.dtype)


def pack(tiles, dest, mu, colb):
    held, rows, cols = tiles.shape
    smem = pl.BlockSpec(memory_space=pltpu.SMEM)
    vmem = pl.BlockSpec(memory_space=pltpu.VMEM)
    return pl.pallas_call(
        pack_kernel,
        out_shape=jax.ShapeDtypeStruct((NX * NY, NZH * CAP * rows + LABEL_ROWS, cols), tiles.dtype),
        in_specs=[smem, smem, smem, vmem],
        out_specs=vmem,
        scratch_shapes=[pltpu.SMEM((NX * NZH * NY,), jnp.int32)],
        compiler_params=pltpu.CompilerParams(vmem_limit_bytes=24 << 20),
        cost_estimate=pl.CostEstimate(flops=0, bytes_accessed=4 << 20, transcendentals=0),
        name="pack",
    )(dest, mu, colb, tiles)


def contract_kernel(labels, plane, arrived, own, other, out, dense):
    rows = 64
    cols = arrived.shape[2]
    slots = NZH * CAP

    @pl.when(pl.program_id(0) == 0)
    def _():
        @pl.loop(0, dense.shape[0] // rows)
        def _(m):
            dense[pl.ds(pl.multiple_of(m * rows, rows), rows), :] = jnp.zeros((rows, dense.shape[1]), dense.dtype)

        @pl.loop(0, NX * NY)
        def _(j):
            for slot in range(slots):
                label = labels[j, slot]

                @pl.when(label > 0)
                def _():
                    cell = label - 1
                    row = pl.multiple_of((cell // CB) * rows, rows)
                    col = pl.multiple_of((slot // CAP * CB + cell % CB) * cols, cols)
                    dense[pl.ds(row, rows), pl.ds(col, cols)] = arrived[j, pl.ds(slot * rows, rows), :]

    width = CB * cols

    def multiply(a):
        for h in range(NZH):
            out[h] = jnp.dot(a[...], dense[:, h * width : (h + 1) * width], preferred_element_type=jnp.float32)

    @pl.when(pl.program_id(0) < NX)
    def _():
        multiply(own)

    @pl.when(pl.program_id(0) >= NX)
    def _():
        multiply(other)


def contract(labels, plane, arrived, own, other):
    occ, mu_rows = own.shape
    cols = arrived.shape[2]
    step = occ // NX

    def rows_of(i, labels, plane):
        return 0, i % NX * NZH + jnp.where(i < NX, plane[0], 1 - plane[0]), 0

    return pl.pallas_call(
        contract_kernel,
        out_shape=jax.ShapeDtypeStruct((NZH, occ * NZH, CB * cols), jnp.float32),
        grid_spec=pltpu.PrefetchScalarGridSpec(
            num_scalar_prefetch=2,
            grid=(NX * NZH,),
            in_specs=[
                pl.BlockSpec(arrived.shape, lambda i, labels, plane: (0, 0, 0)),
                pl.BlockSpec((step, mu_rows), lambda i, labels, plane: (jnp.minimum(i, NX - 1), 0)),
                pl.BlockSpec((step, mu_rows), lambda i, labels, plane: (jnp.maximum(i - NX, 0), 0)),
            ],
            out_specs=pl.BlockSpec((NZH, step, CB * cols), rows_of),
            scratch_shapes=[pltpu.VMEM((mu_rows, NZH * CB * cols), own.dtype)],
        ),
        compiler_params=pltpu.CompilerParams(vmem_limit_bytes=40 << 20),
        cost_estimate=pl.CostEstimate(
            flops=4 * occ * mu_rows * NZH * CB * cols, bytes_accessed=15 << 20, transcendentals=0
        ),
        name="contract",
    )(labels, plane, arrived, own, other)


AXES = ("row", "col")


def per_device(tiles, dest_col, mu_block, col_block, coeff):
    held, rows, cols = tiles.shape[2:]
    plane = (lax.axis_index("col") // NY % NZH).reshape(1)
    mine = coeff.T
    groups = plane_groups()
    swap = [(c, (c // NY // NZH * NZH + 1 - c // NY % NZH) * NY + c % NY) for c in range(NX * NZH * NY)]
    theirs = lax.ppermute(mine, "col", swap)
    own = lax.all_gather(mine, AXES, axis=0, tiled=True, axis_index_groups=groups)
    other = lax.all_gather(theirs, AXES, axis=0, tiled=True, axis_index_groups=groups)
    outgoing = pack(
        tiles.reshape(held, rows, cols), dest_col.reshape(held), mu_block.reshape(held), col_block.reshape(held)
    )
    arrived = lax.all_to_all(outgoing, AXES, split_axis=0, concat_axis=0, tiled=True, axis_index_groups=groups)
    labels = arrived[:, NZH * CAP * rows, : NZH * CAP].astype(jnp.int32)
    share = contract(labels, plane, arrived, own, other)
    share = share.reshape(-1, share.shape[2])
    result = lax.psum_scatter(share, AXES, scatter_dimension=0, tiled=True, axis_index_groups=column_groups())
    return result.astype(jnp.bfloat16)


def solution(mesh):
    in_specs = (
        P("row", "col", None, None, None),
        P("row", "col", None, None),
        P("row", "col", None),
        P("row", "col", None),
        P("row", "col"),
    )
    return jax.shard_map(per_device, mesh=mesh, in_specs=in_specs, out_specs=P("row", "col"), check_vma=False)
```

```python
import jax
import jax.numpy as jnp
from jax import lax
from jax.experimental import pallas as pl
from jax.experimental.pallas import tpu as pltpu
from jax.sharding import PartitionSpec as P

CB = 4
CAP = 2
NX, NZH, NY = 4, 2, 8
NZL, NCORE = 6, 2
N_COL = NX * NZH * NY
LABEL_ROWS = 16
CELLS = 128
GROUP = 8
OUT_ROWS = 128


def device(zl, core, x, zh, y):
    return (((zl * NCORE + core) * NX + x) * NZH + zh) * NY + y


def column(x, zh, y):
    return (x * NZH + zh) * NY + y


X_GROUPS = [[column(x, zh, y) for x in range(NX)] for zh in range(NZH) for y in range(NY)]
Y_GROUPS = [[column(x, zh, y) for y in range(NY)] for x in range(NX) for zh in range(NZH)]
ZL_GROUPS = [[zl * NCORE + core for zl in range(NZL)] for core in range(NCORE)]
PLANE_SWAP = [
    (column(x, zh, y), column(x, 1 - zh, y)) for x in range(NX) for zh in range(NZH) for y in range(NY)
]
CORE_SWAP = [(zl * NCORE + core, zl * NCORE + 1 - core) for zl in range(NZL) for core in range(NCORE)]


def x_shift(by):
    return [
        (column(x, zh, y), column((x + by) % NX, zh, y))
        for x in range(NX)
        for zh in range(NZH)
        for y in range(NY)
    ]


def pack_kernel(route, tiles, out, count):
    held, rows, cols = tiles.shape
    label_at = CAP * rows

    @pl.loop(0, N_COL)
    def _(c):
        count[c] = 0
        out[c, pl.ds(label_at, LABEL_ROWS), :] = jnp.zeros((LABEL_ROWS, cols), out.dtype)

    lane = lax.broadcasted_iota(jnp.int32, (LABEL_ROWS, cols), 1)

    @pl.loop(0, held)
    def _(t):
        c = route[t] // CELLS
        slot = count[c]
        count[c] = slot + 1
        out[c, pl.ds(pl.multiple_of(slot * rows, rows), rows), :] = tiles[t]
        label = (route[t] % CELLS + 1).astype(jnp.float32)
        old = out[c, pl.ds(label_at, LABEL_ROWS), :].astype(jnp.float32)
        out[c, pl.ds(label_at, LABEL_ROWS), :] = jnp.where(lane == slot, label, old).astype(out.dtype)


SMEM = pl.BlockSpec(memory_space=pltpu.SMEM)
VMEM = pl.BlockSpec(memory_space=pltpu.VMEM)
ANY = pl.BlockSpec(memory_space=pl.ANY)


def pack(tiles, route):
    held, rows, cols = tiles.shape
    return pl.pallas_call(
        pack_kernel,
        out_shape=jax.ShapeDtypeStruct((N_COL, CAP * rows + LABEL_ROWS, cols), tiles.dtype),
        in_specs=[SMEM, VMEM],
        out_specs=VMEM,
        scratch_shapes=[pltpu.SMEM((N_COL,), jnp.int32)],
        compiler_params=pltpu.CompilerParams(vmem_limit_bytes=24 << 20),
        cost_estimate=pl.CostEstimate(flops=0, bytes_accessed=4 << 20, transcendentals=0),
        name="pack",
    )(route, tiles)


def place_kernel(labels, arrived, dense):
    rows = (arrived.shape[1] - LABEL_ROWS) // CAP
    cols = arrived.shape[2]

    @pl.loop(0, dense.shape[0] // rows)
    def _(m):
        dense[pl.ds(pl.multiple_of(m * rows, rows), rows), :] = jnp.zeros((rows, dense.shape[1]), dense.dtype)

    @pl.loop(0, N_COL)
    def _(j):
        for slot in range(CAP):
            label = labels[j, slot]

            @pl.when(label > 0)
            def _():
                cell = label - 1
                row = pl.multiple_of((cell // CB) * rows, rows)
                col = pl.multiple_of(cell % CB * cols, cols)
                dense[pl.ds(row, rows), pl.ds(col, cols)] = arrived[j, pl.ds(slot * rows, rows), :]


def place(labels, arrived, mu_rows):
    return pl.pallas_call(
        place_kernel,
        out_shape=jax.ShapeDtypeStruct((mu_rows, CB * arrived.shape[2]), arrived.dtype),
        in_specs=[SMEM, VMEM],
        out_specs=VMEM,
        compiler_params=pltpu.CompilerParams(vmem_limit_bytes=24 << 20),
        cost_estimate=pl.CostEstimate(flops=0, bytes_accessed=4 << 20, transcendentals=0),
        name="place",
    )(labels, arrived)


def contract_kernel(where, own, near, left, right, far0, far1, dense, keep, send, total, sem):
    x, plane, core = where[0], where[1], where[2]
    per = near.shape[0] // NY
    groups = OUT_ROWS // GROUP

    def store(c, block):
        for i in range(per // GROUP):
            g = c * (per // GROUP) + i
            away = jnp.where(g // groups % NCORE == core, 0, 1)
            row = pl.multiple_of((g // (groups * NCORE) * groups + g % groups) * GROUP, GROUP)
            total[away, pl.ds(row, GROUP), :] = block[i * GROUP : (i + 1) * GROUP]

    half = NY // 2
    for h in range(2):
        a = own[h * half : (h + 1) * half].reshape(half * NX * per, own.shape[2])
        product = jnp.dot(a, dense[...], preferred_element_type=jnp.float32)
        for y in range(half):
            for xx in range(NX):
                at = (y * NX + xx) * per
                store((xx * NZH + plane) * NY + h * half + y, product[at : at + per])
    for by, parts in ((0, (near,)), (NX - 1, (left,)), (1, (right,)), (2, (far0, far1))):
        a = parts[0][...] if len(parts) == 1 else jnp.concatenate([p[...] for p in parts], axis=0)
        product = jnp.dot(a, dense[...], preferred_element_type=jnp.float32)
        for y in range(NY):
            store(((x + by) % NX * NZH + 1 - plane) * NY + y, product[y * per : (y + 1) * per])
    copies = [pltpu.make_async_copy(total.at[k], ref, sem.at[k]) for k, ref in enumerate((keep, send))]
    for copy in copies:
        copy.start()
    for copy in copies:
        copy.wait()


def contract(where, own, near, left, right, far0, far1, dense):
    occ = own.shape[0] * own.shape[1] * NZH
    shape = jax.ShapeDtypeStruct((occ // NCORE, dense.shape[1]), jnp.float32)
    return pl.pallas_call(
        contract_kernel,
        out_shape=(shape, shape),
        in_specs=[SMEM] + [VMEM] * 7,
        out_specs=(ANY, ANY),
        scratch_shapes=[
            pltpu.VMEM((NCORE, *shape.shape), jnp.float32),
            pltpu.SemaphoreType.DMA((NCORE,)),
        ],
        compiler_params=pltpu.CompilerParams(vmem_limit_bytes=40 << 20),
        cost_estimate=pl.CostEstimate(
            flops=2 * occ * dense.shape[0] * dense.shape[1], bytes_accessed=12 << 20, transcendentals=0
        ),
        name="contract",
    )(where, own, near, left, right, far0, far1, dense)


def per_device(tiles, dest_col, mu_block, col_block, coeff):
    held, rows, cols = tiles.shape[2:]
    mu_rows, per = coeff.shape
    here = lax.axis_index("col")
    where = jnp.stack([here // (NZH * NY), here // NY % NZH, lax.axis_index("row") % NCORE]).astype(jnp.int32)
    route = dest_col.reshape(held) * CELLS + mu_block.reshape(held) * CB + col_block.reshape(held)
    outgoing = pack(tiles.reshape(held, rows, cols), route)
    outgoing, mine = lax.optimization_barrier((outgoing, coeff.T))
    arrived = lax.all_to_all(outgoing, "col", split_axis=0, concat_axis=0, tiled=True)
    theirs = lax.ppermute(mine, "col", PLANE_SWAP)

    own = lax.all_gather(mine, "col", axis=0, tiled=True, axis_index_groups=X_GROUPS)
    own = lax.all_gather(own, "col", axis=0, tiled=True, axis_index_groups=Y_GROUPS)
    own = own.reshape(NY, NX * per, mu_rows)

    near = lax.all_gather(theirs, "col", axis=0, tiled=True, axis_index_groups=Y_GROUPS)
    left = lax.ppermute(near, "col", x_shift(1))
    right = lax.ppermute(near, "col", x_shift(-1))
    cut = near.shape[0] // 2
    far0 = lax.ppermute(left[:cut], "col", x_shift(1))
    far1 = lax.ppermute(right[cut:], "col", x_shift(-1))

    labels = arrived[:, CAP * rows, :CAP].astype(jnp.int32)
    dense = place(labels, arrived, mu_rows)
    keep, send = contract(where, own, near, left, right, far0, far1, dense)
    share = keep + lax.ppermute(send, "row", CORE_SWAP)
    result = lax.psum_scatter(share, "row", scatter_dimension=0, tiled=True, axis_index_groups=ZL_GROUPS)
    return result.astype(jnp.bfloat16)


def solution(mesh):
    in_specs = (
        P("row", "col", None, None, None),
        P("row", "col", None, None),
        P("row", "col", None),
        P("row", "col", None),
        P("row", "col"),
    )
    return jax.shard_map(per_device, mesh=mesh, in_specs=in_specs, out_specs=P("row", "col"), check_vma=False)
```

```python
import jax
import jax.numpy as jnp
from jax import lax
from jax.experimental import pallas as pl
from jax.experimental.pallas import tpu as pltpu
from jax.sharding import PartitionSpec as P

CB = 4
CAP = 2
NX, NZH, NY = 4, 2, 8
NZL, NCORE = 6, 2
NEAR = NZL // 2
N_COL = NX * NZH * NY
LABEL_ROWS = 16
CELLS = 128
GROUP = 8
OUT_ROWS = 128


def device(zl, core, x, zh, y):
    return (((zl * NCORE + core) * NX + x) * NZH + zh) * NY + y


def column(x, zh, y):
    return (x * NZH + zh) * NY + y


Y_GROUPS = [[column(x, zh, y) for y in range(NY)] for x in range(NX) for zh in range(NZH)]
NEAR_GROUPS = [
    [zl * NCORE + core for zl in range(half * NEAR, (half + 1) * NEAR)]
    for half in range(NZL // NEAR)
    for core in range(NCORE)
]
FAR_SWAP = [
    (zl * NCORE + core, (zl + NEAR) % NZL * NCORE + core) for zl in range(NZL) for core in range(NCORE)
]
PLANE_SWAP = [
    (column(x, zh, y), column(x, 1 - zh, y)) for x in range(NX) for zh in range(NZH) for y in range(NY)
]
CORE_SWAP = [(zl * NCORE + core, zl * NCORE + 1 - core) for zl in range(NZL) for core in range(NCORE)]


def x_shift(by):
    return [
        (column(x, zh, y), column((x + by) % NX, zh, y))
        for x in range(NX)
        for zh in range(NZH)
        for y in range(NY)
    ]


def pack_kernel(route, tiles, out, count):
    held, rows, cols = tiles.shape
    label_at = CAP * rows

    @pl.loop(0, N_COL)
    def _(c):
        count[c] = 0
        out[c, pl.ds(label_at, LABEL_ROWS), :] = jnp.zeros((LABEL_ROWS, cols), out.dtype)

    lane = lax.broadcasted_iota(jnp.int32, (LABEL_ROWS, cols), 1)

    @pl.loop(0, held)
    def _(t):
        c = route[t] // CELLS
        slot = count[c]
        count[c] = slot + 1
        out[c, pl.ds(pl.multiple_of(slot * rows, rows), rows), :] = tiles[t]
        label = (route[t] % CELLS + 1).astype(jnp.float32)
        old = out[c, pl.ds(label_at, LABEL_ROWS), :].astype(jnp.float32)
        out[c, pl.ds(label_at, LABEL_ROWS), :] = jnp.where(lane == slot, label, old).astype(out.dtype)


SMEM = pl.BlockSpec(memory_space=pltpu.SMEM)
VMEM = pl.BlockSpec(memory_space=pltpu.VMEM)
ANY = pl.BlockSpec(memory_space=pl.ANY)


def pack(tiles, route):
    held, rows, cols = tiles.shape
    return pl.pallas_call(
        pack_kernel,
        out_shape=jax.ShapeDtypeStruct((N_COL, CAP * rows + LABEL_ROWS, cols), tiles.dtype),
        in_specs=[SMEM, VMEM],
        out_specs=VMEM,
        scratch_shapes=[pltpu.SMEM((N_COL,), jnp.int32)],
        compiler_params=pltpu.CompilerParams(vmem_limit_bytes=24 << 20),
        cost_estimate=pl.CostEstimate(flops=0, bytes_accessed=4 << 20, transcendentals=0),
        name="pack",
    )(route, tiles)


def place_kernel(labels, arrived, dense):
    rows = (arrived.shape[1] - LABEL_ROWS) // CAP
    cols = arrived.shape[2]

    @pl.loop(0, dense.shape[0] // rows)
    def _(m):
        dense[pl.ds(pl.multiple_of(m * rows, rows), rows), :] = jnp.zeros((rows, dense.shape[1]), dense.dtype)

    @pl.loop(0, N_COL)
    def _(j):
        for slot in range(CAP):
            label = labels[j, slot]

            @pl.when(label > 0)
            def _():
                cell = label - 1
                row = pl.multiple_of((cell // CB) * rows, rows)
                col = pl.multiple_of(cell % CB * cols, cols)
                dense[pl.ds(row, rows), pl.ds(col, cols)] = arrived[j, pl.ds(slot * rows, rows), :]


def place(labels, arrived, mu_rows):
    return pl.pallas_call(
        place_kernel,
        out_shape=jax.ShapeDtypeStruct((mu_rows, CB * arrived.shape[2]), arrived.dtype),
        in_specs=[SMEM, VMEM],
        out_specs=VMEM,
        compiler_params=pltpu.CompilerParams(vmem_limit_bytes=24 << 20),
        cost_estimate=pl.CostEstimate(flops=0, bytes_accessed=4 << 20, transcendentals=0),
        name="place",
    )(labels, arrived)


def contract_kernel(where, own, near, left, right, far0, far1, dense, keep, send, a, b, total, loads, stores):
    x, plane, zl, core = where[0], where[1], where[2], where[3]
    step = near.shape[0]
    per = step // NY
    groups = OUT_ROWS // GROUP

    parts = [(0, near, 0), (1, left, 0), (2, right, 0), (3, far0, 0), (3, far1, far0.shape[0])]
    copies = []
    for n, (slot, ref, at) in enumerate(parts):
        copies.append(pltpu.make_async_copy(ref, b.at[pl.ds(slot * step + at, ref.shape[0])], loads.at[n]))
    copies.append(pltpu.make_async_copy(own, a, loads.at[len(parts)]))
    for copy in copies:
        copy.start()

    def store(c, block):
        for i in range(per // GROUP):
            g = c * (per // GROUP) + i
            away = jnp.where(g // groups % NCORE == core, 0, 1)
            to = g // (groups * NCORE)
            slot = to % NEAR * 2 + jnp.where(to // NEAR == zl // NEAR, 0, 1)
            row = pl.multiple_of((slot * groups + g % groups) * GROUP, GROUP)
            total[away, pl.ds(row, GROUP), :] = block[i * GROUP : (i + 1) * GROUP]

    def multiply(rows, columns):
        product = jnp.dot(rows, dense[...], preferred_element_type=jnp.float32)
        for n, c in enumerate(columns):
            store(c, product[n * per : (n + 1) * per])

    def at_column(by, side, y):
        return ((x + by) % NX * NZH + side) * NY + y

    for copy in copies[:3]:
        copy.wait()
    multiply(b[: 2 * step, :], [at_column(by, 1 - plane, y) for by in (0, NX - 1) for y in range(NY)])
    for copy in copies[3:5]:
        copy.wait()
    multiply(b[2 * step :, :], [at_column(by, 1 - plane, y) for by in (1, 2) for y in range(NY)])
    copies[5].wait()
    half = max(NY // 2, 1)
    for y0 in range(0, NY, half):
        rows = a[y0 * NX * per : (y0 + half) * NX * per, :]
        multiply(rows, [at_column(by, plane, y0 + y) for y in range(half) for by in (0, NX - 1, 1, 2)])
    out = [pltpu.make_async_copy(total.at[k], ref, stores.at[k]) for k, ref in enumerate((keep, send))]
    for copy in out:
        copy.start()
    for copy in out:
        copy.wait()


def contract(where, own, near, left, right, far0, far1, dense):
    occ = own.shape[0] * NZH
    shape = jax.ShapeDtypeStruct((occ // NCORE, dense.shape[1]), jnp.float32)
    return pl.pallas_call(
        contract_kernel,
        out_shape=(shape, shape),
        in_specs=[SMEM] + [ANY] * 6 + [VMEM],
        out_specs=(ANY, ANY),
        scratch_shapes=[
            pltpu.VMEM(own.shape, own.dtype),
            pltpu.VMEM(own.shape, own.dtype),
            pltpu.VMEM((NCORE, *shape.shape), jnp.float32),
            pltpu.SemaphoreType.DMA((6,)),
            pltpu.SemaphoreType.DMA((NCORE,)),
        ],
        compiler_params=pltpu.CompilerParams(vmem_limit_bytes=56 << 20),
        cost_estimate=pl.CostEstimate(
            flops=2 * occ * dense.shape[0] * dense.shape[1], bytes_accessed=12 << 20, transcendentals=0
        ),
        name="contract",
    )(where, own, near, left, right, far0, far1, dense)


def per_device(tiles, dest_col, mu_block, col_block, coeff):
    held, rows, cols = tiles.shape[2:]
    mu_rows, per = coeff.shape
    here, row = lax.axis_index("col"), lax.axis_index("row")
    where = jnp.stack([here // (NZH * NY), here // NY % NZH, row // NCORE, row % NCORE]).astype(jnp.int32)

    mine = coeff.T
    theirs = lax.ppermute(mine, "col", PLANE_SWAP)
    own = jnp.concatenate([mine] + [lax.ppermute(mine, "col", x_shift(by)) for by in (1, -1, 2)], axis=0)
    route = dest_col.reshape(held) * CELLS + mu_block.reshape(held) * CB + col_block.reshape(held)
    outgoing = pack(tiles.reshape(held, rows, cols), route)
    outgoing, theirs, own = lax.optimization_barrier((outgoing, theirs, own))
    arrived = lax.all_to_all(outgoing, "col", split_axis=0, concat_axis=0, tiled=True)

    own = lax.all_gather(own, "col", axis=0, tiled=True, axis_index_groups=Y_GROUPS)
    near = lax.all_gather(theirs, "col", axis=0, tiled=True, axis_index_groups=Y_GROUPS)
    left = lax.ppermute(near, "col", x_shift(1))
    right = lax.ppermute(near, "col", x_shift(-1))
    cut = near.shape[0] // 2
    far0 = lax.ppermute(left[:cut], "col", x_shift(1))
    far1 = lax.ppermute(right[cut:], "col", x_shift(-1))

    labels = arrived[:, CAP * rows, :CAP].astype(jnp.int32)
    dense = place(labels, arrived, mu_rows)
    keep, send = contract(where, own, near, left, right, far0, far1, dense)
    share = keep + lax.ppermute(send, "row", CORE_SWAP)
    share = lax.all_to_all(
        share.reshape(NEAR, 2 * OUT_ROWS, -1), "row", split_axis=0, concat_axis=0, tiled=True, axis_index_groups=NEAR_GROUPS
    )
    away = jnp.sum(share[:, OUT_ROWS:], axis=0)
    result = jnp.sum(share[:, :OUT_ROWS], axis=0) + lax.ppermute(away, "row", FAR_SWAP)
    return result.astype(jnp.bfloat16)


def solution(mesh):
    in_specs = (
        P("row", "col", None, None, None),
        P("row", "col", None, None),
        P("row", "col", None),
        P("row", "col", None),
        P("row", "col"),
    )
    return jax.shard_map(per_device, mesh=mesh, in_specs=in_specs, out_specs=P("row", "col"), check_vma=False)
```

```python
import jax
import jax.numpy as jnp
from jax import lax
from jax.experimental import pallas as pl
from jax.experimental.pallas import tpu as pltpu
from jax.sharding import PartitionSpec as P

CB = 4
CAP = 2
NX, NZH, NY = 4, 2, 8
NZL, NCORE = 6, 2
NEAR = NZL // 2
N_COL = NX * NZH * NY
LABEL_ROWS = 16
CELLS = 128
GROUP = 8
OUT_ROWS = 128
WIDE = 32


def device(zl, core, x, zh, y):
    return (((zl * NCORE + core) * NX + x) * NZH + zh) * NY + y


def column(x, zh, y):
    return (x * NZH + zh) * NY + y


Y_GROUPS = [[column(x, zh, y) for y in range(NY)] for x in range(NX) for zh in range(NZH)]
NEAR_GROUPS = [
    [zl * NCORE + core for zl in range(half * NEAR, (half + 1) * NEAR)]
    for half in range(NZL // NEAR)
    for core in range(NCORE)
]
FAR_SWAP = [
    (zl * NCORE + core, (zl + NEAR) % NZL * NCORE + core) for zl in range(NZL) for core in range(NCORE)
]
PLANE_SWAP = [
    (column(x, zh, y), column(x, 1 - zh, y)) for x in range(NX) for zh in range(NZH) for y in range(NY)
]
CORE_SWAP = [(zl * NCORE + core, zl * NCORE + 1 - core) for zl in range(NZL) for core in range(NCORE)]


def x_shift(by):
    return [
        (column(x, zh, y), column((x + by) % NX, zh, y))
        for x in range(NX)
        for zh in range(NZH)
        for y in range(NY)
    ]


def pack_kernel(route, tiles, out, count):
    held, rows, cols = tiles.shape
    label_at = CAP * rows

    @pl.loop(0, N_COL)
    def _(c):
        count[c] = 0
        out[c, pl.ds(label_at, LABEL_ROWS), :] = jnp.zeros((LABEL_ROWS, cols), out.dtype)

    lane = lax.broadcasted_iota(jnp.int32, (LABEL_ROWS, cols), 1)

    @pl.loop(0, held)
    def _(t):
        c = route[t] // CELLS
        slot = count[c]
        count[c] = slot + 1
        out[c, pl.ds(pl.multiple_of(slot * rows, rows), rows), :] = tiles[t]
        label = (route[t] % CELLS + 1).astype(jnp.float32)
        old = out[c, pl.ds(label_at, LABEL_ROWS), :].astype(jnp.float32)
        out[c, pl.ds(label_at, LABEL_ROWS), :] = jnp.where(lane == slot, label, old).astype(out.dtype)


SMEM = pl.BlockSpec(memory_space=pltpu.SMEM)
VMEM = pl.BlockSpec(memory_space=pltpu.VMEM)
ANY = pl.BlockSpec(memory_space=pl.ANY)


def pack(tiles, route):
    held, rows, cols = tiles.shape
    return pl.pallas_call(
        pack_kernel,
        out_shape=jax.ShapeDtypeStruct((N_COL, CAP * rows + LABEL_ROWS, cols), tiles.dtype),
        in_specs=[SMEM, VMEM],
        out_specs=VMEM,
        scratch_shapes=[pltpu.SMEM((N_COL,), jnp.int32)],
        compiler_params=pltpu.CompilerParams(vmem_limit_bytes=24 << 20),
        cost_estimate=pl.CostEstimate(flops=0, bytes_accessed=4 << 20, transcendentals=0),
        name="pack",
    )(route, tiles)


def place_kernel(labels, arrived, dense):
    rows = (arrived.shape[1] - LABEL_ROWS) // CAP
    cols = arrived.shape[2]

    @pl.loop(0, dense.shape[0] // rows)
    def _(m):
        dense[pl.ds(pl.multiple_of(m * rows, rows), rows), :] = jnp.zeros((rows, dense.shape[1]), dense.dtype)

    @pl.loop(0, N_COL)
    def _(j):
        for slot in range(CAP):
            label = labels[j, slot]

            @pl.when(label > 0)
            def _():
                cell = label - 1
                row = pl.multiple_of((cell // CB) * rows, rows)
                col = pl.multiple_of(cell % CB * cols, cols)
                dense[pl.ds(row, rows), pl.ds(col, cols)] = arrived[j, pl.ds(slot * rows, rows), :]


def place(labels, arrived, mu_rows):
    return pl.pallas_call(
        place_kernel,
        out_shape=jax.ShapeDtypeStruct((mu_rows, CB * arrived.shape[2]), arrived.dtype),
        in_specs=[SMEM, VMEM],
        out_specs=VMEM,
        compiler_params=pltpu.CompilerParams(vmem_limit_bytes=24 << 20),
        cost_estimate=pl.CostEstimate(flops=0, bytes_accessed=4 << 20, transcendentals=0),
        name="place",
    )(labels, arrived)


def contract_kernel(where, near, left, right, far0, far1, dense, keep, send, a, total, loads, stores):
    x, plane, zl, core = where[0], where[1], where[2], where[3]
    step = near.shape[0]
    per = step // (NZH * NY)
    groups = OUT_ROWS // GROUP

    parts = [(0, near), (step, left), (2 * step, right), (3 * step, far0), (3 * step + far0.shape[0], far1)]
    copies = [
        pltpu.make_async_copy(ref, a.at[pl.ds(at, ref.shape[0])], loads.at[n]) for n, (at, ref) in enumerate(parts)
    ]
    for copy in copies:
        copy.start()

    def store(c, block):
        for i in range(per // GROUP):
            g = c * (per // GROUP) + i
            away = jnp.where(g // groups % NCORE == core, 0, 1)
            to = g // (groups * NCORE)
            slot = to % NEAR * 2 + jnp.where(to // NEAR == zl // NEAR, 0, 1)
            row = pl.multiple_of((slot * groups + g % groups) * GROUP, GROUP)
            total[away, pl.ds(row, GROUP), :] = block[i * GROUP : (i + 1) * GROUP]

    for n, by in enumerate((0, NX - 1, 1, 2)):
        for copy in copies[n : n + 1 if n < 3 else n + 2]:
            copy.wait()
        product = jnp.dot(a[n * step : (n + 1) * step, :], dense[...], preferred_element_type=jnp.float32)
        for m, side in enumerate((plane, 1 - plane)):
            for y in range(NY):
                row = (m * NY + y) * per
                store(((x + by) % NX * NZH + side) * NY + y, product[row : row + per])
    out = [pltpu.make_async_copy(total.at[k], ref, stores.at[k]) for k, ref in enumerate((keep, send))]
    for copy in out:
        copy.start()
    for copy in out:
        copy.wait()


def contract(where, near, left, right, far0, far1, dense):
    occ = near.shape[0] * NX
    shape = jax.ShapeDtypeStruct((occ // NCORE, dense.shape[1]), jnp.float32)
    return pl.pallas_call(
        contract_kernel,
        out_shape=(shape, shape),
        in_specs=[SMEM] + [ANY] * 5 + [VMEM],
        out_specs=(ANY, ANY),
        scratch_shapes=[
            pltpu.VMEM((occ, dense.shape[0]), near.dtype),
            pltpu.VMEM((NCORE, *shape.shape), jnp.float32),
            pltpu.SemaphoreType.DMA((5,)),
            pltpu.SemaphoreType.DMA((NCORE,)),
        ],
        compiler_params=pltpu.CompilerParams(vmem_limit_bytes=56 << 20),
        cost_estimate=pl.CostEstimate(
            flops=2 * occ * dense.shape[0] * dense.shape[1], bytes_accessed=12 << 20, transcendentals=0
        ),
        name="contract",
    )(where, near, left, right, far0, far1, dense)


def per_device(tiles, dest_col, mu_block, col_block, coeff):
    held, rows, cols = tiles.shape[2:]
    mu_rows, per = coeff.shape
    here, row = lax.axis_index("col"), lax.axis_index("row")
    where = jnp.stack([here // (NZH * NY), here // NY % NZH, row // NCORE, row % NCORE]).astype(jnp.int32)

    mine = coeff.T
    padded = jnp.pad(mine, ((0, WIDE - per), (0, 0)))
    own = lax.all_gather(padded, "col", axis=0, tiled=True, axis_index_groups=Y_GROUPS)
    own = own.reshape(NY, WIDE, mu_rows)[:, :per].reshape(NY * per, mu_rows)
    theirs = lax.ppermute(mine, "col", PLANE_SWAP)
    route = dest_col.reshape(held) * CELLS + mu_block.reshape(held) * CB + col_block.reshape(held)
    outgoing = pack(tiles.reshape(held, rows, cols), route)
    theirs = lax.all_gather(theirs, "col", axis=0, tiled=True, axis_index_groups=Y_GROUPS)
    near = jnp.concatenate([own, theirs], axis=0)
    outgoing, near = lax.optimization_barrier((outgoing, near))
    arrived = lax.all_to_all(outgoing, "col", split_axis=0, concat_axis=0, tiled=True)

    left = lax.ppermute(near, "col", x_shift(1))
    right = lax.ppermute(near, "col", x_shift(-1))
    cut = near.shape[0] // 2
    far0 = lax.ppermute(left[:cut], "col", x_shift(1))
    far1 = lax.ppermute(right[cut:], "col", x_shift(-1))

    labels = arrived[:, CAP * rows, :CAP].astype(jnp.int32)
    dense = place(labels, arrived, mu_rows)
    keep, send = contract(where, near, left, right, far0, far1, dense)
    share = keep + lax.ppermute(send, "row", CORE_SWAP)
    share = lax.all_to_all(
        share.reshape(NEAR, 2 * OUT_ROWS, -1), "row", split_axis=0, concat_axis=0, tiled=True, axis_index_groups=NEAR_GROUPS
    )
    away = jnp.sum(share[:, OUT_ROWS:], axis=0)
    result = jnp.sum(share[:, :OUT_ROWS], axis=0) + lax.ppermute(away, "row", FAR_SWAP)
    return result.astype(jnp.bfloat16)


def solution(mesh):
    in_specs = (
        P("row", "col", None, None, None),
        P("row", "col", None, None),
        P("row", "col", None),
        P("row", "col", None),
        P("row", "col"),
    )
    return jax.shard_map(per_device, mesh=mesh, in_specs=in_specs, out_specs=P("row", "col"), check_vma=False)
```

```python
import jax
import jax.numpy as jnp
from jax import lax
from jax.experimental import pallas as pl
from jax.experimental.pallas import tpu as pltpu
from jax.sharding import PartitionSpec as P

CB = 4
CAP = 2
NX, NZH, NY = 4, 2, 8
NZL, NCORE = 6, 2
NEAR = NZL // 2
N_COL = NX * NZH * NY
LABEL_ROWS = 16
CELLS = 128
GROUP = 8
OUT_ROWS = 128
WIDE = 32


def device(zl, core, x, zh, y):
    return (((zl * NCORE + core) * NX + x) * NZH + zh) * NY + y


def column(x, zh, y):
    return (x * NZH + zh) * NY + y


X_GROUPS = [[column(x, zh, y) for x in range(NX)] for zh in range(NZH) for y in range(NY)]
Y_GROUPS = [[column(x, zh, y) for y in range(NY)] for x in range(NX) for zh in range(NZH)]
NEAR_GROUPS = [
    [zl * NCORE + core for zl in range(half * NEAR, (half + 1) * NEAR)]
    for half in range(NZL // NEAR)
    for core in range(NCORE)
]
FAR_SWAP = [
    (zl * NCORE + core, (zl + NEAR) % NZL * NCORE + core) for zl in range(NZL) for core in range(NCORE)
]
PLANE_SWAP = [
    (column(x, zh, y), column(x, 1 - zh, y)) for x in range(NX) for zh in range(NZH) for y in range(NY)
]
CORE_SWAP = [(zl * NCORE + core, zl * NCORE + 1 - core) for zl in range(NZL) for core in range(NCORE)]


def x_shift(by):
    return [
        (column(x, zh, y), column((x + by) % NX, zh, y))
        for x in range(NX)
        for zh in range(NZH)
        for y in range(NY)
    ]


def pack_kernel(route, tiles, out, count):
    held, rows, cols = tiles.shape
    label_at = CAP * rows

    @pl.loop(0, N_COL)
    def _(c):
        count[c] = 0
        out[c, pl.ds(label_at, LABEL_ROWS), :] = jnp.zeros((LABEL_ROWS, cols), out.dtype)

    lane = lax.broadcasted_iota(jnp.int32, (LABEL_ROWS, cols), 1)

    @pl.loop(0, held)
    def _(t):
        c = route[t] // CELLS
        slot = count[c]
        count[c] = slot + 1
        out[c, pl.ds(pl.multiple_of(slot * rows, rows), rows), :] = tiles[t]
        label = (route[t] % CELLS + 1).astype(jnp.float32)
        old = out[c, pl.ds(label_at, LABEL_ROWS), :].astype(jnp.float32)
        out[c, pl.ds(label_at, LABEL_ROWS), :] = jnp.where(lane == slot, label, old).astype(out.dtype)


SMEM = pl.BlockSpec(memory_space=pltpu.SMEM)
VMEM = pl.BlockSpec(memory_space=pltpu.VMEM)
ANY = pl.BlockSpec(memory_space=pl.ANY)


def pack(tiles, route):
    held, rows, cols = tiles.shape
    return pl.pallas_call(
        pack_kernel,
        out_shape=jax.ShapeDtypeStruct((N_COL, CAP * rows + LABEL_ROWS, cols), tiles.dtype),
        in_specs=[SMEM, VMEM],
        out_specs=VMEM,
        scratch_shapes=[pltpu.SMEM((N_COL,), jnp.int32)],
        compiler_params=pltpu.CompilerParams(vmem_limit_bytes=24 << 20),
        cost_estimate=pl.CostEstimate(flops=0, bytes_accessed=4 << 20, transcendentals=0),
        name="pack",
    )(route, tiles)


def contract_kernel(where, labels, own, near, left, right, far0, far1, arrived, keep, send, dense, a, b, total, loads, stores):
    x, plane, zl, core = where[0], where[1], where[2], where[3]
    step = near.shape[0]
    per = step // NY
    groups = OUT_ROWS // GROUP

    parts = [(0, near), (step, left), (2 * step, right), (3 * step, far0), (3 * step + far0.shape[0], far1)]
    copies = [
        pltpu.make_async_copy(ref, b.at[pl.ds(at, ref.shape[0])], loads.at[n]) for n, (at, ref) in enumerate(parts)
    ]
    copies.append(pltpu.make_async_copy(own, a, loads.at[len(parts)]))
    for copy in copies:
        copy.start()

    rows = (arrived.shape[1] - LABEL_ROWS) // CAP
    cols = arrived.shape[2]

    @pl.loop(0, dense.shape[0] // rows)
    def _(m):
        dense[pl.ds(pl.multiple_of(m * rows, rows), rows), :] = jnp.zeros((rows, dense.shape[1]), dense.dtype)

    @pl.loop(0, N_COL)
    def _(j):
        for slot in range(CAP):
            label = labels[j, slot]

            @pl.when(label > 0)
            def _():
                cell = label - 1
                row = pl.multiple_of((cell // CB) * rows, rows)
                col = pl.multiple_of(cell % CB * cols, cols)
                dense[pl.ds(row, rows), pl.ds(col, cols)] = arrived[j, pl.ds(slot * rows, rows), :]

    def store(c, block):
        for i in range(per // GROUP):
            g = c * (per // GROUP) + i
            away = jnp.where(g // groups % NCORE == core, 0, 1)
            to = g // (groups * NCORE)
            slot = to % NEAR * 2 + jnp.where(to // NEAR == zl // NEAR, 0, 1)
            row = pl.multiple_of((slot * groups + g % groups) * GROUP, GROUP)
            total[away, pl.ds(row, GROUP), :] = block[i * GROUP : (i + 1) * GROUP]

    def multiply(block, columns, side):
        product = jnp.dot(block, dense[...], preferred_element_type=jnp.float32)
        for n, xx in enumerate(columns):
            for y in range(NY):
                row = n * step + y * per
                store((xx * NZH + side) * NY + y, product[row : row + per])

    for copy in copies:
        copy.wait()
    for n in range(0, NX, 2):
        multiply(a[n * step : (n + 2) * step, :], (n, n + 1), plane)
    multiply(b[: 2 * step, :], (x, (x + NX - 1) % NX), 1 - plane)
    multiply(b[2 * step :, :], ((x + 1) % NX, (x + 2) % NX), 1 - plane)
    out = [pltpu.make_async_copy(total.at[k], ref, stores.at[k]) for k, ref in enumerate((keep, send))]
    for copy in out:
        copy.start()
    for copy in out:
        copy.wait()


def contract(where, labels, own, near, left, right, far0, far1, arrived):
    occ, mu_rows = own.shape[0] * NZH, own.shape[1]
    width = CB * arrived.shape[2]
    shape = jax.ShapeDtypeStruct((occ // NCORE, width), jnp.float32)
    return pl.pallas_call(
        contract_kernel,
        out_shape=(shape, shape),
        in_specs=[SMEM] * 2 + [ANY] * 6 + [VMEM],
        out_specs=(ANY, ANY),
        scratch_shapes=[
            pltpu.VMEM((mu_rows, width), own.dtype),
            pltpu.VMEM(own.shape, own.dtype),
            pltpu.VMEM(own.shape, own.dtype),
            pltpu.VMEM((NCORE, *shape.shape), jnp.float32),
            pltpu.SemaphoreType.DMA((6,)),
            pltpu.SemaphoreType.DMA((NCORE,)),
        ],
        compiler_params=pltpu.CompilerParams(vmem_limit_bytes=56 << 20),
        cost_estimate=pl.CostEstimate(flops=2 * occ * mu_rows * width, bytes_accessed=12 << 20, transcendentals=0),
        name="contract",
    )(where, labels, own, near, left, right, far0, far1, arrived)


def per_device(tiles, dest_col, mu_block, col_block, coeff):
    held, rows, cols = tiles.shape[2:]
    mu_rows, per = coeff.shape
    here, row = lax.axis_index("col"), lax.axis_index("row")
    where = jnp.stack([here // (NZH * NY), here // NY % NZH, row // NCORE, row % NCORE]).astype(jnp.int32)

    mine = coeff.T
    padded = jnp.pad(mine, ((0, WIDE - per), (0, 0)))
    own = lax.all_gather(padded, "col", axis=0, tiled=True, axis_index_groups=Y_GROUPS)
    own = own.reshape(NY, WIDE, mu_rows)[:, :per].reshape(NY * per, mu_rows)
    theirs = lax.ppermute(mine, "col", PLANE_SWAP)
    route = dest_col.reshape(held) * CELLS + mu_block.reshape(held) * CB + col_block.reshape(held)
    outgoing = pack(tiles.reshape(held, rows, cols), route)
    near = lax.all_gather(theirs, "col", axis=0, tiled=True, axis_index_groups=Y_GROUPS)
    outgoing, own, near = lax.optimization_barrier((outgoing, own, near))
    arrived = lax.all_to_all(outgoing, "col", split_axis=0, concat_axis=0, tiled=True)

    own = lax.all_gather(own, "col", axis=0, tiled=True, axis_index_groups=X_GROUPS)
    left = lax.ppermute(near, "col", x_shift(1))
    right = lax.ppermute(near, "col", x_shift(-1))
    cut = near.shape[0] // 2
    far0 = lax.ppermute(left[:cut], "col", x_shift(1))
    far1 = lax.ppermute(right[cut:], "col", x_shift(-1))

    labels = arrived[:, CAP * rows, :CAP].astype(jnp.int32)
    keep, send = contract(where, labels, own, near, left, right, far0, far1, arrived)
    share = keep + lax.ppermute(send, "row", CORE_SWAP)
    share = lax.all_to_all(
        share.reshape(NEAR, 2 * OUT_ROWS, -1), "row", split_axis=0, concat_axis=0, tiled=True, axis_index_groups=NEAR_GROUPS
    )
    away = jnp.sum(share[:, OUT_ROWS:], axis=0)
    result = jnp.sum(share[:, :OUT_ROWS], axis=0) + lax.ppermute(away, "row", FAR_SWAP)
    return result.astype(jnp.bfloat16)


def solution(mesh):
    in_specs = (
        P("row", "col", None, None, None),
        P("row", "col", None, None),
        P("row", "col", None),
        P("row", "col", None),
        P("row", "col"),
    )
    return jax.shard_map(per_device, mesh=mesh, in_specs=in_specs, out_specs=P("row", "col"), check_vma=False)
```

```python
import functools

import jax
import jax.numpy as jnp
from jax import lax
from jax.experimental import pallas as pl
from jax.experimental.pallas import tpu as pltpu
from jax.sharding import PartitionSpec as P

CB = 4
CAP = 2
NX, NZH, NY = 4, 2, 8
NZL, NCORE = 6, 2
NEAR = NZL // 2
N_COL = NX * NZH * NY
LABEL_ROWS = 16
CELLS = 128
GROUP = 8
HALF = 64
WIDE = 32


def device(zl, core, x, zh, y):
    return (((zl * NCORE + core) * NX + x) * NZH + zh) * NY + y


def column(x, zh, y):
    return (x * NZH + zh) * NY + y


Y_GROUPS = [[column(x, zh, y) for y in range(NY)] for x in range(NX) for zh in range(NZH)]
NEAR_GROUPS = [
    [zl * NCORE + core for zl in range(half * NEAR, (half + 1) * NEAR)]
    for half in range(NZL // NEAR)
    for core in range(NCORE)
]
SIDE_SWAP = [(3 * m + a, 3 * m + 2 - a) for m in range(NZL * NCORE // 3) for a in (0, 2)]
FAR_SWAP = [
    (zl * NCORE + core, (zl + NEAR) % NZL * NCORE + core) for zl in range(NZL) for core in range(NCORE)
]
PLANE_SWAP = [
    (column(x, zh, y), column(x, 1 - zh, y)) for x in range(NX) for zh in range(NZH) for y in range(NY)
]
CORE_SWAP = [(zl * NCORE + core, zl * NCORE + 1 - core) for zl in range(NZL) for core in range(NCORE)]


def x_shift(by):
    return [
        (column(x, zh, y), column((x + by) % NX, zh, y))
        for x in range(NX)
        for zh in range(NZH)
        for y in range(NY)
    ]


def pack_kernel(route, tiles, out, count):
    held, rows, cols = tiles.shape
    label_at = CAP * rows

    @pl.loop(0, N_COL)
    def _(c):
        count[c] = 0
        out[c, pl.ds(label_at, LABEL_ROWS), :] = jnp.zeros((LABEL_ROWS, cols), out.dtype)

    lane = lax.broadcasted_iota(jnp.int32, (LABEL_ROWS, cols), 1)

    @pl.loop(0, held)
    def _(t):
        c = route[t] // CELLS
        slot = count[c]
        count[c] = slot + 1
        out[c, pl.ds(pl.multiple_of(slot * rows, rows), rows), :] = tiles[t]
        label = (route[t] % CELLS + 1).astype(jnp.float32)
        old = out[c, pl.ds(label_at, LABEL_ROWS), :].astype(jnp.float32)
        out[c, pl.ds(label_at, LABEL_ROWS), :] = jnp.where(lane == slot, label, old).astype(out.dtype)


SMEM = pl.BlockSpec(memory_space=pltpu.SMEM)
VMEM = pl.BlockSpec(memory_space=pltpu.VMEM)
ANY = pl.BlockSpec(memory_space=pl.ANY)


def pack(tiles, route):
    held, rows, cols = tiles.shape
    return pl.pallas_call(
        pack_kernel,
        out_shape=jax.ShapeDtypeStruct((N_COL, CAP * rows + LABEL_ROWS, cols), tiles.dtype),
        in_specs=[SMEM, VMEM],
        out_specs=VMEM,
        scratch_shapes=[pltpu.SMEM((N_COL,), jnp.int32)],
        compiler_params=pltpu.CompilerParams(vmem_limit_bytes=24 << 20),
        cost_estimate=pl.CostEstimate(flops=0, bytes_accessed=4 << 20, transcendentals=0),
        name="pack",
    )(route, tiles)


def assigned_row(u):
    q = u % 6
    return u // 6 * 3 + jnp.where(q == 1, 2, jnp.where(q == 5, 0, q // 2))


def contract_kernel(first, where, *refs):
    if first:
        labels, near, left, right, far0, far1, arrived, keep, send, dense, a, total, loads, stores = refs
    else:
        near, left, right, far0, far1, dense, keep, send, a, total, loads, stores = refs
    x, plane, zl, core = where[0], where[1], where[2], where[3]
    side = plane if first else 1 - plane
    step = near.shape[0]
    per = step // NY
    groups = HALF // GROUP

    parts = [(0, near), (step, left), (2 * step, right), (3 * step, far0), (3 * step + far0.shape[0], far1)]
    copies = [
        pltpu.make_async_copy(ref, a.at[pl.ds(at, ref.shape[0])], loads.at[n]) for n, (at, ref) in enumerate(parts)
    ]
    for copy in copies:
        copy.start()

    if first:
        rows = (arrived.shape[1] - LABEL_ROWS) // CAP
        cols = arrived.shape[2]

        @pl.loop(0, dense.shape[0] // rows)
        def _(m):
            dense[pl.ds(pl.multiple_of(m * rows, rows), rows), :] = jnp.zeros((rows, dense.shape[1]), dense.dtype)

        @pl.loop(0, N_COL)
        def _(j):
            for slot in range(CAP):
                label = labels[j, slot]

                @pl.when(label > 0)
                def _():
                    cell = label - 1
                    row = pl.multiple_of((cell // CB) * rows, rows)
                    col = pl.multiple_of(cell % CB * cols, cols)
                    dense[pl.ds(row, rows), pl.ds(col, cols)] = arrived[j, pl.ds(slot * rows, rows), :]

    def store(c, block):
        for i in range(per // GROUP):
            g = c * (per // GROUP) + i
            to = assigned_row(g // groups)
            away = jnp.where(to % NCORE == core, 0, 1)
            to = to // NCORE
            slot = to % NEAR * 2 + jnp.where(to // NEAR == zl // NEAR, 0, 1)
            row = pl.multiple_of((slot * groups + g % groups) * GROUP, GROUP)
            total[away, pl.ds(row, GROUP), :] = block[i * GROUP : (i + 1) * GROUP]

    def multiply(block, columns):
        product = jnp.dot(block, dense[...], preferred_element_type=jnp.float32)
        for n, xx in enumerate(columns):
            for y in range(NY):
                row = n * step + y * per
                store((xx * NZH + side) * NY + y, product[row : row + per])

    for copy in copies:
        copy.wait()
    multiply(a[: 2 * step, :], (x, (x + NX - 1) % NX))
    multiply(a[2 * step :, :], ((x + 1) % NX, (x + 2) % NX))
    out = [pltpu.make_async_copy(total.at[k], ref, stores.at[k]) for k, ref in enumerate((keep, send))]
    for copy in out:
        copy.start()
    for copy in out:
        copy.wait()


def contract(where, parts, dense=None, labels=None, arrived=None):
    first = dense is None
    step, mu_rows = parts[0].shape
    occ = step * NX
    width = CB * arrived.shape[2] if first else dense.shape[1]
    shape = jax.ShapeDtypeStruct((occ // NCORE, width), jnp.float32)
    placed = jax.ShapeDtypeStruct((mu_rows, width), parts[0].dtype)
    return pl.pallas_call(
        functools.partial(contract_kernel, first),
        out_shape=(shape, shape, placed) if first else (shape, shape),
        in_specs=[SMEM] * (2 if first else 1) + [ANY] * 5 + [VMEM],
        out_specs=(ANY, ANY, VMEM) if first else (ANY, ANY),
        scratch_shapes=[
            pltpu.VMEM((occ, mu_rows), parts[0].dtype),
            pltpu.VMEM((NCORE, *shape.shape), jnp.float32),
            pltpu.SemaphoreType.DMA((5,)),
            pltpu.SemaphoreType.DMA((NCORE,)),
        ],
        compiler_params=pltpu.CompilerParams(vmem_limit_bytes=56 << 20),
        cost_estimate=pl.CostEstimate(flops=2 * occ * mu_rows * width, bytes_accessed=8 << 20, transcendentals=0),
        name="contract",
    )(where, *([labels] if first else []), *parts, arrived if first else dense)


def along_y(rows):
    per, mu_rows = rows.shape
    padded = jnp.pad(rows, ((0, WIDE - per), (0, 0)))
    gathered = lax.all_gather(padded, "col", axis=0, tiled=True, axis_index_groups=Y_GROUPS)
    return gathered.reshape(NY, WIDE, mu_rows)[:, :per].reshape(NY * per, mu_rows)


def along_x(near):
    left = lax.ppermute(near, "col", x_shift(1))
    right = lax.ppermute(near, "col", x_shift(-1))
    cut = near.shape[0] // 2
    far0 = lax.ppermute(left[:cut], "col", x_shift(1))
    far1 = lax.ppermute(right[cut:], "col", x_shift(-1))
    return near, left, right, far0, far1


def swap_cores(keep, send):
    return keep + lax.ppermute(send, "row", CORE_SWAP)


def reduce(share):
    share = lax.all_to_all(
        share.reshape(NEAR, 2 * HALF, -1), "row", split_axis=0, concat_axis=0, tiled=True, axis_index_groups=NEAR_GROUPS
    )
    away = jnp.sum(share[:, HALF:], axis=0)
    result = jnp.sum(share[:, :HALF], axis=0) + lax.ppermute(away, "row", FAR_SWAP)
    return result.astype(jnp.bfloat16)


def per_device(tiles, dest_col, mu_block, col_block, coeff):
    held, rows, cols = tiles.shape[2:]
    here, row = lax.axis_index("col"), lax.axis_index("row")
    plane = here // NY % NZH
    where = jnp.stack([here // (NZH * NY), plane, row // NCORE, row % NCORE]).astype(jnp.int32)

    mine = coeff.T
    theirs = lax.ppermute(mine, "col", PLANE_SWAP)
    own = lax.all_gather(mine, "col", axis=0, tiled=True, axis_index_groups=Y_GROUPS)
    route = dest_col.reshape(held) * CELLS + mu_block.reshape(held) * CB + col_block.reshape(held)
    outgoing = pack(tiles.reshape(held, rows, cols), route)
    outgoing, own, theirs = lax.optimization_barrier((outgoing, own, theirs))
    arrived = lax.all_to_all(outgoing, "col", split_axis=0, concat_axis=0, tiled=True)
    labels = arrived[:, CAP * rows, :CAP].astype(jnp.int32)

    keep, send, dense = contract(where, along_x(own), labels=labels, arrived=arrived)
    share = swap_cores(keep, send)
    own_sum = reduce(share)
    parts = along_x(along_y(theirs))
    dense, _ = lax.optimization_barrier((dense, share))
    their_sum = reduce(swap_cores(*contract(where, parts, dense=dense)))

    side0 = jnp.where(plane == 0, own_sum, their_sum)
    side1 = jnp.where(plane == 0, their_sum, own_sum)
    moved = lax.ppermute(jnp.where(row % 3 == 0, side1, side0), "row", SIDE_SWAP)
    top = jnp.where(row % 3 == 2, side1, side0)
    return jnp.concatenate([top, jnp.where(row % 3 == 1, side1, moved)], axis=0)


def solution(mesh):
    in_specs = (
        P("row", "col", None, None, None),
        P("row", "col", None, None),
        P("row", "col", None),
        P("row", "col", None),
        P("row", "col"),
    )
    return jax.shard_map(per_device, mesh=mesh, in_specs=in_specs, out_specs=P("row", "col"), check_vma=False)
```

```python
import jax
import jax.numpy as jnp
from jax import lax
from jax.experimental import pallas as pl
from jax.experimental.pallas import tpu as pltpu
from jax.sharding import PartitionSpec as P

CB = 4
CAP = 2
NX, NZH, NY = 4, 2, 8
NZL, NCORE = 6, 2
NEAR = NZL // 2
N_COL = NX * NZH * NY
LABEL_ROWS = 16
CELLS = 128
GROUP = 8
OUT_ROWS = 128
WIDE = 32


def device(zl, core, x, zh, y):
    return (((zl * NCORE + core) * NX + x) * NZH + zh) * NY + y


def column(x, zh, y):
    return (x * NZH + zh) * NY + y


Y_GROUPS = [[column(x, zh, y) for y in range(NY)] for x in range(NX) for zh in range(NZH)]
FAR_SWAP = [
    (zl * NCORE + core, (zl + NEAR) % NZL * NCORE + core) for zl in range(NZL) for core in range(NCORE)
]
PLANE_SWAP = [
    (column(x, zh, y), column(x, 1 - zh, y)) for x in range(NX) for zh in range(NZH) for y in range(NY)
]
CORE_SWAP = [(zl * NCORE + core, zl * NCORE + 1 - core) for zl in range(NZL) for core in range(NCORE)]


def near_shift(by):
    return [
        (zl * NCORE + core, (zl // NEAR * NEAR + (zl + by) % NEAR) * NCORE + core)
        for zl in range(NZL)
        for core in range(NCORE)
    ]


def x_shift(by):
    return [
        (column(x, zh, y), column((x + by) % NX, zh, y))
        for x in range(NX)
        for zh in range(NZH)
        for y in range(NY)
    ]


def pack_kernel(route, tiles, out, count):
    held, rows, cols = tiles.shape
    label_at = CAP * rows

    @pl.loop(0, N_COL)
    def _(c):
        count[c] = 0
        out[c, pl.ds(label_at, LABEL_ROWS), :] = jnp.zeros((LABEL_ROWS, cols), out.dtype)

    lane = lax.broadcasted_iota(jnp.int32, (LABEL_ROWS, cols), 1)

    @pl.loop(0, held)
    def _(t):
        c = route[t] // CELLS
        slot = count[c]
        count[c] = slot + 1
        out[c, pl.ds(pl.multiple_of(slot * rows, rows), rows), :] = tiles[t]
        label = (route[t] % CELLS + 1).astype(jnp.float32)
        old = out[c, pl.ds(label_at, LABEL_ROWS), :].astype(jnp.float32)
        out[c, pl.ds(label_at, LABEL_ROWS), :] = jnp.where(lane == slot, label, old).astype(out.dtype)


SMEM = pl.BlockSpec(memory_space=pltpu.SMEM)
VMEM = pl.BlockSpec(memory_space=pltpu.VMEM)
ANY = pl.BlockSpec(memory_space=pl.ANY)


def pack(tiles, route):
    held, rows, cols = tiles.shape
    return pl.pallas_call(
        pack_kernel,
        out_shape=jax.ShapeDtypeStruct((N_COL, CAP * rows + LABEL_ROWS, cols), tiles.dtype),
        in_specs=[SMEM, VMEM],
        out_specs=VMEM,
        scratch_shapes=[pltpu.SMEM((N_COL,), jnp.int32)],
        compiler_params=pltpu.CompilerParams(vmem_limit_bytes=24 << 20),
        cost_estimate=pl.CostEstimate(flops=0, bytes_accessed=4 << 20, transcendentals=0),
        name="pack",
    )(route, tiles)


def contract_kernel(where, labels, *refs):
    parts, (arrived, keep, send, dense, a, total, loads, stores) = refs[:-8], refs[-8:]
    x, plane, zl, core = where[0], where[1], where[2], where[3]
    step = parts[0].shape[0]
    per = step // NY
    groups = OUT_ROWS // GROUP

    copies, at = [], 0
    for n, ref in enumerate(parts):
        copies.append(pltpu.make_async_copy(ref, a.at[pl.ds(at, ref.shape[0])], loads.at[n]))
        at += ref.shape[0]
    for copy in copies:
        copy.start()

    rows = (arrived.shape[1] - LABEL_ROWS) // CAP
    cols = arrived.shape[2]

    @pl.loop(0, dense.shape[0] // rows)
    def _(m):
        dense[pl.ds(pl.multiple_of(m * rows, rows), rows), :] = jnp.zeros((rows, dense.shape[1]), dense.dtype)

    @pl.loop(0, N_COL)
    def _(j):
        for slot in range(CAP):
            label = labels[j, slot]

            @pl.when(label > 0)
            def _():
                cell = label - 1
                row = pl.multiple_of((cell // CB) * rows, rows)
                col = pl.multiple_of(cell % CB * cols, cols)
                dense[pl.ds(row, rows), pl.ds(col, cols)] = arrived[j, pl.ds(slot * rows, rows), :]

    def store(c, block):
        for i in range(per // GROUP):
            g = c * (per // GROUP) + i
            away = jnp.where(g // groups % NCORE == core, 0, 1)
            to = g // (groups * NCORE)
            slot = (to + NEAR - zl % NEAR) % NEAR * 2 + jnp.where(to // NEAR == zl // NEAR, 0, 1)
            row = pl.multiple_of((slot * groups + g % groups) * GROUP, GROUP)
            total[away, pl.ds(row, GROUP), :] = block[i * GROUP : (i + 1) * GROUP]

    def multiply(block, shifts, side):
        product = jnp.dot(block, dense[...], preferred_element_type=jnp.float32)
        for n, by in enumerate(shifts):
            for y in range(NY):
                row = n * step + y * per
                store(((x + by) % NX * NZH + side) * NY + y, product[row : row + per])

    for copy in copies:
        copy.wait()
    for n, side in enumerate((plane, 1 - plane)):
        for m, shifts in enumerate(((0, NX - 1), (1, 2))):
            at = (n * NX + m * 2) * step
            multiply(a[at : at + 2 * step, :], shifts, side)
    out = [pltpu.make_async_copy(total.at[k], ref, stores.at[k]) for k, ref in enumerate((keep, send))]
    for copy in out:
        copy.start()
    for copy in out:
        copy.wait()


def contract(where, labels, parts, arrived):
    step, mu_rows = parts[0].shape
    occ = step * NX * NZH
    width = CB * arrived.shape[2]
    shape = jax.ShapeDtypeStruct((occ // NCORE, width), jnp.float32)
    return pl.pallas_call(
        contract_kernel,
        out_shape=(shape, shape),
        in_specs=[SMEM] * 2 + [ANY] * len(parts) + [VMEM],
        out_specs=(ANY, ANY),
        scratch_shapes=[
            pltpu.VMEM((mu_rows, width), parts[0].dtype),
            pltpu.VMEM((occ, mu_rows), parts[0].dtype),
            pltpu.VMEM((NCORE, *shape.shape), jnp.float32),
            pltpu.SemaphoreType.DMA((len(parts),)),
            pltpu.SemaphoreType.DMA((NCORE,)),
        ],
        compiler_params=pltpu.CompilerParams(vmem_limit_bytes=56 << 20),
        cost_estimate=pl.CostEstimate(flops=2 * occ * mu_rows * width, bytes_accessed=12 << 20, transcendentals=0),
        name="contract",
    )(where, labels, *parts, arrived)


def beside(near):
    return lax.ppermute(near, "col", x_shift(1)), lax.ppermute(near, "col", x_shift(-1))


def across(left, right):
    cut = left.shape[0] // 2
    return lax.ppermute(left[:cut], "col", x_shift(1)), lax.ppermute(right[cut:], "col", x_shift(-1))


def per_device(tiles, dest_col, mu_block, col_block, coeff):
    held, rows, cols = tiles.shape[2:]
    mu_rows, per = coeff.shape
    here, row = lax.axis_index("col"), lax.axis_index("row")
    where = jnp.stack([here // (NZH * NY), here // NY % NZH, row // NCORE, row % NCORE]).astype(jnp.int32)

    mine = coeff.T
    padded = jnp.pad(lax.ppermute(mine, "col", PLANE_SWAP), ((0, WIDE - per), (0, 0)))
    theirs = lax.all_gather(padded, "col", axis=0, tiled=True, axis_index_groups=Y_GROUPS)
    theirs = theirs.reshape(NY, WIDE, mu_rows)[:, :per].reshape(NY * per, mu_rows)
    own = lax.all_gather(mine, "col", axis=0, tiled=True, axis_index_groups=Y_GROUPS)
    left, right = beside(own)
    route = dest_col.reshape(held) * CELLS + mu_block.reshape(held) * CB + col_block.reshape(held)
    outgoing = pack(tiles.reshape(held, rows, cols), route)
    outgoing, theirs, left, right = lax.optimization_barrier((outgoing, theirs, left, right))
    arrived = lax.all_to_all(outgoing, "col", split_axis=0, concat_axis=0, tiled=True)

    parts = [own, left, right, *across(left, right)]
    left, right = beside(theirs)
    parts += [theirs, left, right, *across(left, right)]

    labels = arrived[:, CAP * rows, :CAP].astype(jnp.int32)
    keep, send = contract(where, labels, parts, arrived)
    share = keep + lax.ppermute(send, "row", CORE_SWAP)
    share = share.reshape(NEAR, 2 * OUT_ROWS, -1)
    here, *others = [share[0]] + [lax.ppermute(share[by], "row", near_shift(by)) for by in range(1, NEAR)]
    away = sum((part[OUT_ROWS:] for part in others), here[OUT_ROWS:])
    result = sum((part[:OUT_ROWS] for part in others), here[:OUT_ROWS])
    result = result + lax.ppermute(away, "row", FAR_SWAP)
    return result.astype(jnp.bfloat16)


def solution(mesh):
    in_specs = (
        P("row", "col", None, None, None),
        P("row", "col", None, None),
        P("row", "col", None),
        P("row", "col", None),
        P("row", "col"),
    )
    return jax.shard_map(per_device, mesh=mesh, in_specs=in_specs, out_specs=P("row", "col"), check_vma=False)
```

```python
import jax
import jax.numpy as jnp
from jax import lax
from jax.experimental import pallas as pl
from jax.experimental.pallas import tpu as pltpu
from jax.sharding import PartitionSpec as P

CB = 4
CAP = 2
NX, NZH, NY = 4, 2, 8
NZL, NCORE = 6, 2
NEAR = NZL // 2
N_COL = NX * NZH * NY
LABEL_ROWS = 16
CELLS = 128
GROUP = 8
OUT_ROWS = 128
WIDE = 32


def device(zl, core, x, zh, y):
    return (((zl * NCORE + core) * NX + x) * NZH + zh) * NY + y


def column(x, zh, y):
    return (x * NZH + zh) * NY + y


Y_GROUPS = [[column(x, zh, y) for y in range(NY)] for x in range(NX) for zh in range(NZH)]
NEAR_GROUPS = [
    [zl * NCORE + core for zl in range(half * NEAR, (half + 1) * NEAR)]
    for half in range(NZL // NEAR)
    for core in range(NCORE)
]
FAR_SWAP = [
    (zl * NCORE + core, (zl + NEAR) % NZL * NCORE + core) for zl in range(NZL) for core in range(NCORE)
]
PLANE_SWAP = [
    (column(x, zh, y), column(x, 1 - zh, y)) for x in range(NX) for zh in range(NZH) for y in range(NY)
]
CORE_SWAP = [(zl * NCORE + core, zl * NCORE + 1 - core) for zl in range(NZL) for core in range(NCORE)]


def x_shift(by):
    return [
        (column(x, zh, y), column((x + by) % NX, zh, y))
        for x in range(NX)
        for zh in range(NZH)
        for y in range(NY)
    ]


def pack_kernel(route, tiles, out, count):
    held, rows, cols = tiles.shape
    label_at = CAP * rows

    @pl.loop(0, N_COL)
    def _(c):
        count[c] = 0
        out[c, pl.ds(label_at, LABEL_ROWS), :] = jnp.zeros((LABEL_ROWS, cols), out.dtype)

    lane = lax.broadcasted_iota(jnp.int32, (LABEL_ROWS, cols), 1)

    @pl.loop(0, held)
    def _(t):
        c = route[t] // CELLS
        slot = count[c]
        count[c] = slot + 1
        out[c, pl.ds(pl.multiple_of(slot * rows, rows), rows), :] = tiles[t]
        label = (route[t] % CELLS + 1).astype(jnp.float32)
        old = out[c, pl.ds(label_at, LABEL_ROWS), :].astype(jnp.float32)
        out[c, pl.ds(label_at, LABEL_ROWS), :] = jnp.where(lane == slot, label, old).astype(out.dtype)


SMEM = pl.BlockSpec(memory_space=pltpu.SMEM)
VMEM = pl.BlockSpec(memory_space=pltpu.VMEM)
ANY = pl.BlockSpec(memory_space=pl.ANY)


def pack(tiles, route):
    held, rows, cols = tiles.shape
    return pl.pallas_call(
        pack_kernel,
        out_shape=jax.ShapeDtypeStruct((N_COL, CAP * rows + LABEL_ROWS, cols), tiles.dtype),
        in_specs=[SMEM, VMEM],
        out_specs=VMEM,
        scratch_shapes=[pltpu.SMEM((N_COL,), jnp.int32)],
        compiler_params=pltpu.CompilerParams(vmem_limit_bytes=24 << 20),
        cost_estimate=pl.CostEstimate(flops=0, bytes_accessed=4 << 20, transcendentals=0),
        name="pack",
    )(route, tiles)


def contract_kernel(where, labels, *refs):
    parts, (arrived, keep, send, dense, a, total, loads, stores) = refs[:-8], refs[-8:]
    x, plane, zl, core = where[0], where[1], where[2], where[3]
    step = parts[0].shape[0]
    per = step // NY
    groups = OUT_ROWS // GROUP

    copies, at = [], 0
    for n, ref in enumerate(parts):
        copies.append(pltpu.make_async_copy(ref, a.at[pl.ds(at, ref.shape[0])], loads.at[n]))
        at += ref.shape[0]
    for copy in copies:
        copy.start()

    rows = (arrived.shape[1] - LABEL_ROWS) // CAP
    cols = arrived.shape[2]

    @pl.loop(0, dense.shape[0] // rows)
    def _(m):
        dense[pl.ds(pl.multiple_of(m * rows, rows), rows), :] = jnp.zeros((rows, dense.shape[1]), dense.dtype)

    @pl.loop(0, N_COL)
    def _(j):
        for slot in range(CAP):
            label = labels[j, slot]

            @pl.when(label > 0)
            def _():
                cell = label - 1
                row = pl.multiple_of((cell // CB) * rows, rows)
                col = pl.multiple_of(cell % CB * cols, cols)
                dense[pl.ds(row, rows), pl.ds(col, cols)] = arrived[j, pl.ds(slot * rows, rows), :]

    def store(c, block):
        for i in range(per // GROUP):
            g = c * (per // GROUP) + i
            away = jnp.where(g // groups % NCORE == core, 0, 1)
            to = g // (groups * NCORE)
            slot = to % NEAR * 2 + jnp.where(to // NEAR == zl // NEAR, 0, 1)
            row = pl.multiple_of((slot * groups + g % groups) * GROUP, GROUP)
            total[away, pl.ds(row, GROUP), :] = block[i * GROUP : (i + 1) * GROUP]

    def multiply(block, shifts, side):
        product = jnp.dot(block, dense[...], preferred_element_type=jnp.float32)
        for n, by in enumerate(shifts):
            for y in range(NY):
                row = n * step + y * per
                store(((x + by) % NX * NZH + side) * NY + y, product[row : row + per])

    for copy in copies:
        copy.wait()
    for n, side in enumerate((plane, 1 - plane)):
        for m, shifts in enumerate(((0, NX - 1), (1, 2))):
            at = (n * NX + m * 2) * step
            multiply(a[at : at + 2 * step, :], shifts, side)
    out = [pltpu.make_async_copy(total.at[k], ref, stores.at[k]) for k, ref in enumerate((keep, send))]
    for copy in out:
        copy.start()
    for copy in out:
        copy.wait()


def contract(where, labels, parts, arrived):
    step, mu_rows = parts[0].shape
    occ = step * NX * NZH
    width = CB * arrived.shape[2]
    shape = jax.ShapeDtypeStruct((occ // NCORE, width), jnp.float32)
    return pl.pallas_call(
        contract_kernel,
        out_shape=(shape, shape),
        in_specs=[SMEM] * 2 + [ANY] * len(parts) + [VMEM],
        out_specs=(ANY, ANY),
        scratch_shapes=[
            pltpu.VMEM((mu_rows, width), parts[0].dtype),
            pltpu.VMEM((occ, mu_rows), parts[0].dtype),
            pltpu.VMEM((NCORE, *shape.shape), jnp.float32),
            pltpu.SemaphoreType.DMA((len(parts),)),
            pltpu.SemaphoreType.DMA((NCORE,)),
        ],
        compiler_params=pltpu.CompilerParams(vmem_limit_bytes=56 << 20),
        cost_estimate=pl.CostEstimate(flops=2 * occ * mu_rows * width, bytes_accessed=12 << 20, transcendentals=0),
        name="contract",
    )(where, labels, *parts, arrived)


def beside(near):
    return lax.ppermute(near, "col", x_shift(1)), lax.ppermute(near, "col", x_shift(-1))


def across(left, right):
    cut = left.shape[0] // 2
    return lax.ppermute(left[:cut], "col", x_shift(1)), lax.ppermute(right[cut:], "col", x_shift(-1))


def per_device(tiles, dest_col, mu_block, col_block, coeff):
    held, rows, cols = tiles.shape[2:]
    mu_rows, per = coeff.shape
    here, row = lax.axis_index("col"), lax.axis_index("row")
    where = jnp.stack([here // (NZH * NY), here // NY % NZH, row // NCORE, row % NCORE]).astype(jnp.int32)

    mine = coeff.T
    theirs = lax.ppermute(mine, "col", PLANE_SWAP)
    route = dest_col.reshape(held) * CELLS + mu_block.reshape(held) * CB + col_block.reshape(held)
    outgoing = pack(tiles.reshape(held, rows, cols), route)
    outgoing, mine, theirs = lax.optimization_barrier((outgoing, mine, theirs))
    arrived = lax.all_to_all(outgoing, "col", split_axis=0, concat_axis=0, tiled=True)

    padded = jnp.pad(theirs, ((0, WIDE - per), (0, 0)))
    theirs = lax.all_gather(padded, "col", axis=0, tiled=True, axis_index_groups=Y_GROUPS)
    theirs = theirs.reshape(NY, WIDE, mu_rows)[:, :per].reshape(NY * per, mu_rows)
    own = lax.all_gather(mine, "col", axis=0, tiled=True, axis_index_groups=Y_GROUPS)
    parts = []
    for near in (own, theirs):
        left, right = beside(near)
        parts += [near, left, right, *across(left, right)]

    labels = arrived[:, CAP * rows, :CAP].astype(jnp.int32)
    keep, send = contract(where, labels, parts, arrived)
    share = keep + lax.ppermute(send, "row", CORE_SWAP)
    share = lax.all_to_all(
        share.reshape(NEAR, 2 * OUT_ROWS, -1), "row", split_axis=0, concat_axis=0, tiled=True, axis_index_groups=NEAR_GROUPS
    )
    away = jnp.sum(share[:, OUT_ROWS:], axis=0)
    result = jnp.sum(share[:, :OUT_ROWS], axis=0) + lax.ppermute(away, "row", FAR_SWAP)
    return result.astype(jnp.bfloat16)


def solution(mesh):
    in_specs = (
        P("row", "col", None, None, None),
        P("row", "col", None, None),
        P("row", "col", None),
        P("row", "col", None),
        P("row", "col"),
    )
    return jax.shard_map(per_device, mesh=mesh, in_specs=in_specs, out_specs=P("row", "col"), check_vma=False)
```

```python
import jax
import jax.numpy as jnp
from jax import lax
from jax.experimental import pallas as pl
from jax.experimental.pallas import tpu as pltpu
from jax.sharding import PartitionSpec as P

CB = 4
CAP = 2
NX, NZH, NY = 4, 2, 8
NZL, NCORE = 6, 2
NEAR = NZL // 2
N_COL = NX * NZH * NY
LABEL_ROWS = 8
TILE_ROWS = 16
CELLS = 128
GROUP = 8
OUT_ROWS = 128
WIDE = 32


def device(zl, core, x, zh, y):
    return (((zl * NCORE + core) * NX + x) * NZH + zh) * NY + y


def column(x, zh, y):
    return (x * NZH + zh) * NY + y


X_GROUPS = [[column(x, zh, y) for x in range(NX)] for zh in range(NZH) for y in range(NY)]
Y_GROUPS = [[column(x, zh, y) for y in range(NY)] for x in range(NX) for zh in range(NZH)]
NEAR_GROUPS = [
    [zl * NCORE + core for zl in range(half * NEAR, (half + 1) * NEAR)]
    for half in range(NZL // NEAR)
    for core in range(NCORE)
]
FAR_SWAP = [
    (zl * NCORE + core, (zl + NEAR) % NZL * NCORE + core) for zl in range(NZL) for core in range(NCORE)
]
PLANE_SWAP = [
    (column(x, zh, y), column(x, 1 - zh, y)) for x in range(NX) for zh in range(NZH) for y in range(NY)
]
CORE_SWAP = [(zl * NCORE + core, zl * NCORE + 1 - core) for zl in range(NZL) for core in range(NCORE)]


def x_shift(by):
    return [
        (column(x, zh, y), column((x + by) % NX, zh, y))
        for x in range(NX)
        for zh in range(NZH)
        for y in range(NY)
    ]


def pack_kernel(route, tiles, out, labels, count):
    held, rows, cols = tiles.shape

    @pl.loop(0, N_COL)
    def _(c):
        count[c] = 0
        labels[c] = jnp.zeros((TILE_ROWS, cols), labels.dtype)

    lane = lax.broadcasted_iota(jnp.int32, (TILE_ROWS, cols), 1)

    @pl.loop(0, held)
    def _(t):
        c = route[t] // CELLS
        slot = count[c]
        count[c] = slot + 1
        out[c, pl.ds(pl.multiple_of(slot * rows, rows), rows), :] = tiles[t]
        label = (route[t] % CELLS + 1).astype(jnp.float32)
        labels[c] = jnp.where(lane == slot, label, labels[c].astype(jnp.float32)).astype(labels.dtype)


SMEM = pl.BlockSpec(memory_space=pltpu.SMEM)
VMEM = pl.BlockSpec(memory_space=pltpu.VMEM)
ANY = pl.BlockSpec(memory_space=pl.ANY)


def pack(tiles, route):
    held, rows, cols = tiles.shape
    out, labels = pl.pallas_call(
        pack_kernel,
        out_shape=(
            jax.ShapeDtypeStruct((N_COL, CAP * rows + LABEL_ROWS, cols), tiles.dtype),
            jax.ShapeDtypeStruct((N_COL, TILE_ROWS, cols), tiles.dtype),
        ),
        in_specs=[SMEM, VMEM],
        out_specs=(VMEM, VMEM),
        scratch_shapes=[pltpu.SMEM((N_COL,), jnp.int32)],
        compiler_params=pltpu.CompilerParams(vmem_limit_bytes=24 << 20),
        cost_estimate=pl.CostEstimate(flops=0, bytes_accessed=4 << 20, transcendentals=0),
        name="pack",
    )(route, tiles)
    return out.at[:, CAP * rows :].set(labels[:, :LABEL_ROWS])


def place_kernel(labels, arrived, dense):
    rows = (arrived.shape[1] - LABEL_ROWS) // CAP
    cols = arrived.shape[2]

    @pl.loop(0, dense.shape[0] // rows)
    def _(m):
        dense[pl.ds(pl.multiple_of(m * rows, rows), rows), :] = jnp.zeros((rows, dense.shape[1]), dense.dtype)

    @pl.loop(0, N_COL)
    def _(j):
        for slot in range(CAP):
            label = labels[j, slot]

            @pl.when(label > 0)
            def _():
                cell = label - 1
                row = pl.multiple_of((cell // CB) * rows, rows)
                col = pl.multiple_of(cell % CB * cols, cols)
                dense[pl.ds(row, rows), pl.ds(col, cols)] = arrived[j, pl.ds(slot * rows, rows), :]


def place(labels, arrived, mu_rows):
    return pl.pallas_call(
        place_kernel,
        out_shape=jax.ShapeDtypeStruct((mu_rows, CB * arrived.shape[2]), arrived.dtype),
        in_specs=[SMEM, VMEM],
        out_specs=VMEM,
        compiler_params=pltpu.CompilerParams(vmem_limit_bytes=24 << 20),
        cost_estimate=pl.CostEstimate(flops=0, bytes_accessed=4 << 20, transcendentals=0),
        name="place",
    )(labels, arrived)


def contract_kernel(where, own, near, left, right, far0, far1, dense, keep, send, a, b, total, loads, stores):
    x, plane, zl, core = where[0], where[1], where[2], where[3]
    step = near.shape[0]
    per = step // NY
    groups = OUT_ROWS // GROUP

    parts = [(0, near), (step, left), (2 * step, right), (3 * step, far0), (3 * step + far0.shape[0], far1)]
    copies = [
        pltpu.make_async_copy(ref, b.at[pl.ds(at, ref.shape[0])], loads.at[n]) for n, (at, ref) in enumerate(parts)
    ]
    copies.append(pltpu.make_async_copy(own, a, loads.at[len(parts)]))
    for copy in copies:
        copy.start()

    def store(c, block):
        for i in range(per // GROUP):
            g = c * (per // GROUP) + i
            away = jnp.where(g // groups % NCORE == core, 0, 1)
            to = g // (groups * NCORE)
            slot = to % NEAR * 2 + jnp.where(to // NEAR == zl // NEAR, 0, 1)
            row = pl.multiple_of((slot * groups + g % groups) * GROUP, GROUP)
            total[away, pl.ds(row, GROUP), :] = block[i * GROUP : (i + 1) * GROUP]

    def multiply(block, columns, side):
        product = jnp.dot(block, dense[...], preferred_element_type=jnp.float32)
        for n, xx in enumerate(columns):
            for y in range(NY):
                row = n * step + y * per
                store((xx * NZH + side) * NY + y, product[row : row + per])

    for copy in copies[:3]:
        copy.wait()
    multiply(b[: 2 * step, :], (x, (x + NX - 1) % NX), 1 - plane)
    for copy in copies[3:5]:
        copy.wait()
    multiply(b[2 * step :, :], ((x + 1) % NX, (x + 2) % NX), 1 - plane)
    copies[5].wait()
    for n in range(0, NX, 2):
        multiply(a[n * step : (n + 2) * step, :], (n, n + 1), plane)
    out = [pltpu.make_async_copy(total.at[k], ref, stores.at[k]) for k, ref in enumerate((keep, send))]
    for copy in out:
        copy.start()
    for copy in out:
        copy.wait()


def contract(where, own, near, left, right, far0, far1, dense):
    occ, (mu_rows, width) = own.shape[0] * NZH, dense.shape
    shape = jax.ShapeDtypeStruct((occ // NCORE, width), jnp.float32)
    return pl.pallas_call(
        contract_kernel,
        out_shape=(shape, shape),
        in_specs=[SMEM] + [ANY] * 6 + [VMEM],
        out_specs=(ANY, ANY),
        scratch_shapes=[
            pltpu.VMEM(own.shape, own.dtype),
            pltpu.VMEM(own.shape, own.dtype),
            pltpu.VMEM((NCORE, *shape.shape), jnp.float32),
            pltpu.SemaphoreType.DMA((6,)),
            pltpu.SemaphoreType.DMA((NCORE,)),
        ],
        compiler_params=pltpu.CompilerParams(vmem_limit_bytes=56 << 20),
        cost_estimate=pl.CostEstimate(flops=2 * occ * mu_rows * width, bytes_accessed=12 << 20, transcendentals=0),
        name="contract",
    )(where, own, near, left, right, far0, far1, dense)


def per_device(tiles, dest_col, mu_block, col_block, coeff):
    held, rows, cols = tiles.shape[2:]
    mu_rows, per = coeff.shape
    here, row = lax.axis_index("col"), lax.axis_index("row")
    where = jnp.stack([here // (NZH * NY), here // NY % NZH, row // NCORE, row % NCORE]).astype(jnp.int32)

    mine = coeff.T
    padded = jnp.pad(mine, ((0, WIDE - per), (0, 0)))
    own = lax.all_gather(padded, "col", axis=0, tiled=True, axis_index_groups=Y_GROUPS)
    theirs = lax.ppermute(mine, "col", PLANE_SWAP)
    route = dest_col.reshape(held) * CELLS + mu_block.reshape(held) * CB + col_block.reshape(held)
    outgoing = pack(tiles.reshape(held, rows, cols), route)
    near = lax.all_gather(theirs, "col", axis=0, tiled=True, axis_index_groups=Y_GROUPS)
    outgoing, own, near = lax.optimization_barrier((outgoing, own, near))
    arrived = lax.all_to_all(outgoing, "col", split_axis=0, concat_axis=0, tiled=True)

    own = own.reshape(NY, WIDE, mu_rows)[:, :per].reshape(NY * per, mu_rows)
    own = lax.all_gather(own, "col", axis=0, tiled=True, axis_index_groups=X_GROUPS)
    left = lax.ppermute(near, "col", x_shift(1))
    right = lax.ppermute(near, "col", x_shift(-1))
    cut = near.shape[0] // 2
    far0 = lax.ppermute(left[:cut], "col", x_shift(1))
    far1 = lax.ppermute(right[cut:], "col", x_shift(-1))

    labels = arrived[:, CAP * rows, :CAP].astype(jnp.int32)
    dense = place(labels, arrived, mu_rows)
    keep, send = contract(where, own, near, left, right, far0, far1, dense)
    share = keep + lax.ppermute(send, "row", CORE_SWAP)
    share = lax.all_to_all(
        share.reshape(NEAR, 2 * OUT_ROWS, -1), "row", split_axis=0, concat_axis=0, tiled=True, axis_index_groups=NEAR_GROUPS
    )
    away = jnp.sum(share[:, OUT_ROWS:], axis=0)
    result = jnp.sum(share[:, :OUT_ROWS], axis=0) + lax.ppermute(away, "row", FAR_SWAP)
    return result.astype(jnp.bfloat16)


def solution(mesh):
    in_specs = (
        P("row", "col", None, None, None),
        P("row", "col", None, None),
        P("row", "col", None),
        P("row", "col", None),
        P("row", "col"),
    )
    return jax.shard_map(per_device, mesh=mesh, in_specs=in_specs, out_specs=P("row", "col"), check_vma=False)
```

```python
import jax
import jax.numpy as jnp
from jax import lax
from jax.experimental import pallas as pl
from jax.experimental.pallas import tpu as pltpu
from jax.sharding import PartitionSpec as P

CB = 4
CAP = 2
NX, NZH, NY = 4, 2, 8
NZL, NCORE = 6, 2
NEAR = NZL // 2
AXES = ("row", "col")
N_COL = NX * NZH * NY
LABEL_ROWS = 8
TILE_ROWS = 16
CELLS = 128
GROUP = 8
OUT_ROWS = 128
WIDE = 32


def device(zl, core, x, zh, y):
    return (((zl * NCORE + core) * NX + x) * NZH + zh) * NY + y


def column(x, zh, y):
    return (x * NZH + zh) * NY + y


X_GROUPS = [[column(x, zh, y) for x in range(NX)] for zh in range(NZH) for y in range(NY)]
Y_GROUPS = [[column(x, zh, y) for y in range(NY)] for x in range(NX) for zh in range(NZH)]
PLANE_GROUPS = [[column(x, zh, y) for x in range(NX) for y in range(NY)] for zh in range(NZH)]
NEAR_GROUPS = [
    [zl * NCORE + core for zl in range(half * NEAR, (half + 1) * NEAR)]
    for half in range(NZL // NEAR)
    for core in range(NCORE)
]
FAR_SWAP = [
    (zl * NCORE + core, (zl + NEAR) % NZL * NCORE + core) for zl in range(NZL) for core in range(NCORE)
]
PLANE_SWAP = [
    (column(x, zh, y), column(x, 1 - zh, y)) for x in range(NX) for zh in range(NZH) for y in range(NY)
]
CORE_SWAP = [(zl * NCORE + core, zl * NCORE + 1 - core) for zl in range(NZL) for core in range(NCORE)]


def z_shift(by):
    return [
        (device(z % NZL, core, x, z // NZL, y), device(to % NZL, core, x, to // NZL, y))
        for z, to in ((z, (z + by) % (NZL * NZH)) for z in range(NZL * NZH))
        for core in range(NCORE)
        for x in range(NX)
        for y in range(NY)
    ]


def x_shift(by):
    return [
        (column(x, zh, y), column((x + by) % NX, zh, y))
        for x in range(NX)
        for zh in range(NZH)
        for y in range(NY)
    ]


def pack_kernel(where, route, tiles, stay, cross, stay_labels, cross_labels, count):
    held, rows, cols = tiles.shape

    @pl.loop(0, N_COL)
    def _(c):
        count[c] = 0

    @pl.loop(0, NX * NY)
    def _(j):
        stay_labels[j] = jnp.zeros((TILE_ROWS, cols), stay_labels.dtype)
        cross_labels[j] = jnp.zeros((TILE_ROWS, cols), cross_labels.dtype)

    lane = lax.broadcasted_iota(jnp.int32, (TILE_ROWS, cols), 1)

    @pl.loop(0, held)
    def _(t):
        c = route[t] // CELLS
        slot = count[c]
        count[c] = slot + 1
        j = c // (NZH * NY) * NY + c % NY
        label = (route[t] % CELLS + 1).astype(jnp.float32)
        here = c // NY % NZH == where[1]

        def put(out, labels):
            out[j, pl.ds(pl.multiple_of(slot * rows, rows), rows), :] = tiles[t]
            labels[j] = jnp.where(lane == slot, label, labels[j].astype(jnp.float32)).astype(labels.dtype)

        @pl.when(here)
        def _():
            put(stay, stay_labels)

        @pl.when(jnp.logical_not(here))
        def _():
            put(cross, cross_labels)


SMEM = pl.BlockSpec(memory_space=pltpu.SMEM)
VMEM = pl.BlockSpec(memory_space=pltpu.VMEM)
ANY = pl.BlockSpec(memory_space=pl.ANY)


def pack(where, tiles, route):
    held, rows, cols = tiles.shape
    out = jax.ShapeDtypeStruct((NX * NY, CAP * rows + LABEL_ROWS, cols), tiles.dtype)
    labels = jax.ShapeDtypeStruct((NX * NY, TILE_ROWS, cols), tiles.dtype)
    *blocks, label0, label1 = pl.pallas_call(
        pack_kernel,
        out_shape=(out, out, labels, labels),
        in_specs=[SMEM, SMEM, VMEM],
        out_specs=(VMEM,) * 4,
        scratch_shapes=[pltpu.SMEM((N_COL,), jnp.int32)],
        compiler_params=pltpu.CompilerParams(vmem_limit_bytes=24 << 20),
        cost_estimate=pl.CostEstimate(flops=0, bytes_accessed=4 << 20, transcendentals=0),
        name="pack",
    )(where, route, tiles)
    return [
        block.at[:, CAP * rows :].set(label[:, :LABEL_ROWS]) for block, label in zip(blocks, (label0, label1))
    ]


def place_kernel(labels0, labels1, arrived0, arrived1, dense):
    rows = (arrived0.shape[1] - LABEL_ROWS) // CAP
    cols = arrived0.shape[2]

    @pl.loop(0, dense.shape[0] // rows)
    def _(m):
        dense[pl.ds(pl.multiple_of(m * rows, rows), rows), :] = jnp.zeros((rows, dense.shape[1]), dense.dtype)

    @pl.loop(0, NX * NY)
    def _(j):
        for labels, arrived in ((labels0, arrived0), (labels1, arrived1)):
            for slot in range(CAP):
                label = labels[j, slot]

                @pl.when(label > 0)
                def _():
                    cell = label - 1
                    row = pl.multiple_of((cell // CB) * rows, rows)
                    col = pl.multiple_of(cell % CB * cols, cols)
                    dense[pl.ds(row, rows), pl.ds(col, cols)] = arrived[j, pl.ds(slot * rows, rows), :]


def place(labels, arrived, mu_rows):
    return pl.pallas_call(
        place_kernel,
        out_shape=jax.ShapeDtypeStruct((mu_rows, CB * arrived[0].shape[2]), arrived[0].dtype),
        in_specs=[SMEM, SMEM, VMEM, VMEM],
        out_specs=VMEM,
        compiler_params=pltpu.CompilerParams(vmem_limit_bytes=24 << 20),
        cost_estimate=pl.CostEstimate(flops=0, bytes_accessed=4 << 20, transcendentals=0),
        name="place",
    )(*labels, *arrived)


def contract_kernel(where, own, near, left, right, far0, far1, dense, keep, send, a, b, total, loads, stores):
    x, plane, zl, core = where[0], where[1], where[2], where[3]
    step = near.shape[0]
    per = step // NY
    groups = OUT_ROWS // GROUP

    parts = [(0, near), (step, left), (2 * step, right), (3 * step, far0), (3 * step + far0.shape[0], far1)]
    copies = [
        pltpu.make_async_copy(ref, b.at[pl.ds(at, ref.shape[0])], loads.at[n]) for n, (at, ref) in enumerate(parts)
    ]
    copies.append(pltpu.make_async_copy(own, a, loads.at[len(parts)]))
    for copy in copies:
        copy.start()

    def store(c, block):
        for i in range(per // GROUP):
            g = c * (per // GROUP) + i
            away = jnp.where(g // groups % NCORE == core, 0, 1)
            to = g // (groups * NCORE)
            slot = to % NEAR * 2 + jnp.where(to // NEAR == zl // NEAR, 0, 1)
            row = pl.multiple_of((slot * groups + g % groups) * GROUP, GROUP)
            total[away, pl.ds(row, GROUP), :] = block[i * GROUP : (i + 1) * GROUP]

    def multiply(block, columns, side):
        product = jnp.dot(block, dense[...], preferred_element_type=jnp.float32)
        for n, xx in enumerate(columns):
            for y in range(NY):
                row = n * step + y * per
                store((xx * NZH + side) * NY + y, product[row : row + per])

    for copy in copies[:3]:
        copy.wait()
    multiply(b[: 2 * step, :], (x, (x + NX - 1) % NX), 1 - plane)
    for copy in copies[3:5]:
        copy.wait()
    multiply(b[2 * step :, :], ((x + 1) % NX, (x + 2) % NX), 1 - plane)
    copies[5].wait()
    for n in range(0, NX, 2):
        multiply(a[n * step : (n + 2) * step, :], (n, n + 1), plane)
    out = [pltpu.make_async_copy(total.at[k], ref, stores.at[k]) for k, ref in enumerate((keep, send))]
    for copy in out:
        copy.start()
    for copy in out:
        copy.wait()


def contract(where, own, near, left, right, far0, far1, dense):
    occ, (mu_rows, width) = own.shape[0] * NZH, dense.shape
    shape = jax.ShapeDtypeStruct((occ // NCORE, width), jnp.float32)
    return pl.pallas_call(
        contract_kernel,
        out_shape=(shape, shape),
        in_specs=[SMEM] + [ANY] * 6 + [VMEM],
        out_specs=(ANY, ANY),
        scratch_shapes=[
            pltpu.VMEM(own.shape, own.dtype),
            pltpu.VMEM(own.shape, own.dtype),
            pltpu.VMEM((NCORE, *shape.shape), jnp.float32),
            pltpu.SemaphoreType.DMA((6,)),
            pltpu.SemaphoreType.DMA((NCORE,)),
        ],
        compiler_params=pltpu.CompilerParams(vmem_limit_bytes=56 << 20),
        cost_estimate=pl.CostEstimate(flops=2 * occ * mu_rows * width, bytes_accessed=12 << 20, transcendentals=0),
        name="contract",
    )(where, own, near, left, right, far0, far1, dense)


def per_device(tiles, dest_col, mu_block, col_block, coeff):
    held, rows, cols = tiles.shape[2:]
    mu_rows, per = coeff.shape
    here, row = lax.axis_index("col"), lax.axis_index("row")
    where = jnp.stack([here // (NZH * NY), here // NY % NZH, row // NCORE, row % NCORE]).astype(jnp.int32)

    mine = coeff.T
    padded = jnp.pad(mine, ((0, WIDE - per), (0, 0)))
    own = lax.all_gather(padded, "col", axis=0, tiled=True, axis_index_groups=Y_GROUPS)
    theirs = lax.ppermute(mine, "col", PLANE_SWAP)
    route = dest_col.reshape(held) * CELLS + mu_block.reshape(held) * CB + col_block.reshape(held)
    stay, cross = pack(where, tiles.reshape(held, rows, cols), route)
    cut = cross.shape[0] // 2
    over = [lax.ppermute(half, AXES, z_shift(by)) for half, by in ((cross[:cut], NEAR), (cross[cut:], -NEAR))]
    near = lax.all_gather(theirs, "col", axis=0, tiled=True, axis_index_groups=Y_GROUPS)
    stay, own, near, over = lax.optimization_barrier((stay, own, near, over))
    over = [lax.ppermute(half, AXES, z_shift(by)) for half, by in zip(over, (NZL - NEAR, NEAR - NZL))]
    arrived0 = lax.all_to_all(stay, "col", split_axis=0, concat_axis=0, tiled=True, axis_index_groups=PLANE_GROUPS)
    left = lax.ppermute(near, "col", x_shift(1))
    right = lax.ppermute(near, "col", x_shift(-1))
    cross = jnp.concatenate(over, axis=0)
    cross, arrived0, left, right = lax.optimization_barrier((cross, arrived0, left, right))
    arrived1 = lax.all_to_all(cross, "col", split_axis=0, concat_axis=0, tiled=True, axis_index_groups=PLANE_GROUPS)
    arrived = [arrived0, arrived1]

    own = own.reshape(NY, WIDE, mu_rows)[:, :per].reshape(NY * per, mu_rows)
    own = lax.all_gather(own, "col", axis=0, tiled=True, axis_index_groups=X_GROUPS)
    cut = near.shape[0] // 2
    far0 = lax.ppermute(left[:cut], "col", x_shift(1))
    far1 = lax.ppermute(right[cut:], "col", x_shift(-1))

    labels = [part[:, CAP * rows, :CAP].astype(jnp.int32) for part in arrived]
    dense = place(labels, arrived, mu_rows)
    keep, send = contract(where, own, near, left, right, far0, far1, dense)
    share = keep + lax.ppermute(send, "row", CORE_SWAP)
    share = lax.all_to_all(
        share.reshape(NEAR, 2 * OUT_ROWS, -1), "row", split_axis=0, concat_axis=0, tiled=True, axis_index_groups=NEAR_GROUPS
    )
    away = jnp.sum(share[:, OUT_ROWS:], axis=0)
    result = jnp.sum(share[:, :OUT_ROWS], axis=0) + lax.ppermute(away, "row", FAR_SWAP)
    return result.astype(jnp.bfloat16)


def solution(mesh):
    in_specs = (
        P("row", "col", None, None, None),
        P("row", "col", None, None),
        P("row", "col", None),
        P("row", "col", None),
        P("row", "col"),
    )
    return jax.shard_map(per_device, mesh=mesh, in_specs=in_specs, out_specs=P("row", "col"), check_vma=False)
```

```python
import jax
import jax.numpy as jnp
from jax import lax
from jax.experimental import pallas as pl
from jax.experimental.pallas import tpu as pltpu
from jax.sharding import PartitionSpec as P

CB = 4
CAP = 2
NX, NZH, NY = 4, 2, 8
NZL, NCORE = 6, 2
NEAR = NZL // 2
N_COL = NX * NZH * NY
LABEL_ROWS = 8
TILE_ROWS = 16
CELLS = 128
GROUP = 8
OUT_ROWS = 128
WIDE = 32


def device(zl, core, x, zh, y):
    return (((zl * NCORE + core) * NX + x) * NZH + zh) * NY + y


def column(x, zh, y):
    return (x * NZH + zh) * NY + y


X_GROUPS = [[column(x, zh, y) for x in range(NX)] for zh in range(NZH) for y in range(NY)]
Y_GROUPS = [[column(x, zh, y) for y in range(NY)] for x in range(NX) for zh in range(NZH)]
NEAR_GROUPS = [
    [zl * NCORE + core for zl in range(half * NEAR, (half + 1) * NEAR)]
    for half in range(NZL // NEAR)
    for core in range(NCORE)
]
FAR_SWAP = [
    (zl * NCORE + core, (zl + NEAR) % NZL * NCORE + core) for zl in range(NZL) for core in range(NCORE)
]
PLANE_SWAP = [
    (column(x, zh, y), column(x, 1 - zh, y)) for x in range(NX) for zh in range(NZH) for y in range(NY)
]
CORE_SWAP = [(zl * NCORE + core, zl * NCORE + 1 - core) for zl in range(NZL) for core in range(NCORE)]


def x_shift(by):
    return [
        (column(x, zh, y), column((x + by) % NX, zh, y))
        for x in range(NX)
        for zh in range(NZH)
        for y in range(NY)
    ]


def pack_kernel(route, tiles, out, labels, count):
    held, rows, cols = tiles.shape

    @pl.loop(0, N_COL)
    def _(c):
        count[c] = 0
        labels[c] = jnp.zeros((TILE_ROWS, cols), labels.dtype)

    lane = lax.broadcasted_iota(jnp.int32, (TILE_ROWS, cols), 1)

    @pl.loop(0, held)
    def _(t):
        c = route[t] // CELLS
        slot = count[c]
        count[c] = slot + 1
        out[c, pl.ds(pl.multiple_of(slot * rows, rows), rows), :] = tiles[t]
        label = (route[t] % CELLS + 1).astype(jnp.float32)
        labels[c] = jnp.where(lane == slot, label, labels[c].astype(jnp.float32)).astype(labels.dtype)


SMEM = pl.BlockSpec(memory_space=pltpu.SMEM)
VMEM = pl.BlockSpec(memory_space=pltpu.VMEM)
ANY = pl.BlockSpec(memory_space=pl.ANY)


def pack(tiles, route):
    held, rows, cols = tiles.shape
    out, labels = pl.pallas_call(
        pack_kernel,
        out_shape=(
            jax.ShapeDtypeStruct((N_COL, CAP * rows + LABEL_ROWS, cols), tiles.dtype),
            jax.ShapeDtypeStruct((N_COL, TILE_ROWS, cols), tiles.dtype),
        ),
        in_specs=[SMEM, VMEM],
        out_specs=(VMEM, VMEM),
        scratch_shapes=[pltpu.SMEM((N_COL,), jnp.int32)],
        compiler_params=pltpu.CompilerParams(vmem_limit_bytes=24 << 20),
        cost_estimate=pl.CostEstimate(flops=0, bytes_accessed=4 << 20, transcendentals=0),
        name="pack",
    )(route, tiles)
    return out.at[:, CAP * rows :].set(labels[:, :LABEL_ROWS])


def place_kernel(labels, arrived, out, dense, sem):
    rows = (arrived.shape[1] - LABEL_ROWS) // CAP
    cols = arrived.shape[2]

    @pl.loop(0, dense.shape[0] // rows)
    def _(m):
        dense[pl.ds(pl.multiple_of(m * rows, rows), rows), :] = jnp.zeros((rows, dense.shape[1]), dense.dtype)

    @pl.loop(0, N_COL)
    def _(j):
        for slot in range(CAP):
            label = labels[j, slot]

            @pl.when(label > 0)
            def _():
                cell = label - 1
                row = pl.multiple_of((cell // CB) * rows, rows)
                col = pl.multiple_of(cell % CB * cols, cols)
                dense[pl.ds(row, rows), pl.ds(col, cols)] = arrived[j, pl.ds(slot * rows, rows), :]

    copy = pltpu.make_async_copy(dense, out, sem)
    copy.start()
    copy.wait()


def place(labels, arrived, mu_rows):
    shape = jax.ShapeDtypeStruct((mu_rows, CB * arrived.shape[2]), arrived.dtype)
    return pl.pallas_call(
        place_kernel,
        out_shape=shape,
        in_specs=[SMEM, VMEM],
        out_specs=ANY,
        scratch_shapes=[pltpu.VMEM(shape.shape, shape.dtype), pltpu.SemaphoreType.DMA(())],
        compiler_params=pltpu.CompilerParams(vmem_limit_bytes=56 << 20),
        cost_estimate=pl.CostEstimate(flops=0, bytes_accessed=4 << 20, transcendentals=0),
        name="place",
    )(labels, arrived)


def contract_kernel(where, own, near, left, right, far0, far1, dense, keep, send, a, b, total, loads, stores):
    x, plane, zl, core = where[0], where[1], where[2], where[3]
    step = near.shape[0]
    per = step // NY
    groups = OUT_ROWS // GROUP

    parts = [(0, near), (step, left), (2 * step, right), (3 * step, far0), (3 * step + far0.shape[0], far1)]
    copies = [
        pltpu.make_async_copy(ref, b.at[pl.ds(at, ref.shape[0])], loads.at[n]) for n, (at, ref) in enumerate(parts)
    ]
    copies.append(pltpu.make_async_copy(own, a, loads.at[len(parts)]))
    for copy in copies:
        copy.start()

    def store(c, block):
        for i in range(per // GROUP):
            g = c * (per // GROUP) + i
            away = jnp.where(g // groups % NCORE == core, 0, 1)
            to = g // (groups * NCORE)
            slot = to % NEAR * 2 + jnp.where(to // NEAR == zl // NEAR, 0, 1)
            row = pl.multiple_of((slot * groups + g % groups) * GROUP, GROUP)
            total[away, pl.ds(row, GROUP), :] = block[i * GROUP : (i + 1) * GROUP]

    def multiply(block, columns, side):
        product = jnp.dot(block, dense[...], preferred_element_type=jnp.float32)
        for n, xx in enumerate(columns):
            for y in range(NY):
                row = n * step + y * per
                store((xx * NZH + side) * NY + y, product[row : row + per])

    for copy in copies[:3]:
        copy.wait()
    multiply(b[: 2 * step, :], (x, (x + NX - 1) % NX), 1 - plane)
    for copy in copies[3:5]:
        copy.wait()
    multiply(b[2 * step :, :], ((x + 1) % NX, (x + 2) % NX), 1 - plane)
    copies[5].wait()
    for n in range(0, NX, 2):
        multiply(a[n * step : (n + 2) * step, :], (n, n + 1), plane)
    out = [pltpu.make_async_copy(total.at[k], ref, stores.at[k]) for k, ref in enumerate((keep, send))]
    for copy in out:
        copy.start()
    for copy in out:
        copy.wait()


def contract(where, own, near, left, right, far0, far1, dense):
    occ, (mu_rows, width) = own.shape[0] * NZH, dense.shape
    shape = jax.ShapeDtypeStruct((occ // NCORE, width), jnp.float32)
    return pl.pallas_call(
        contract_kernel,
        out_shape=(shape, shape),
        in_specs=[SMEM] + [ANY] * 6 + [VMEM],
        out_specs=(ANY, ANY),
        scratch_shapes=[
            pltpu.VMEM(own.shape, own.dtype),
            pltpu.VMEM(own.shape, own.dtype),
            pltpu.VMEM((NCORE, *shape.shape), jnp.float32),
            pltpu.SemaphoreType.DMA((6,)),
            pltpu.SemaphoreType.DMA((NCORE,)),
        ],
        compiler_params=pltpu.CompilerParams(vmem_limit_bytes=52 << 20),
        cost_estimate=pl.CostEstimate(flops=2 * occ * mu_rows * width, bytes_accessed=12 << 20, transcendentals=0),
        name="contract",
    )(where, own, near, left, right, far0, far1, dense)


def per_device(tiles, dest_col, mu_block, col_block, coeff):
    held, rows, cols = tiles.shape[2:]
    mu_rows, per = coeff.shape
    here, row = lax.axis_index("col"), lax.axis_index("row")
    where = jnp.stack([here // (NZH * NY), here // NY % NZH, row // NCORE, row % NCORE]).astype(jnp.int32)

    mine = coeff.T
    padded = jnp.pad(mine, ((0, WIDE - per), (0, 0)))
    own = lax.all_gather(padded, "col", axis=0, tiled=True, axis_index_groups=Y_GROUPS)
    theirs = lax.ppermute(mine, "col", PLANE_SWAP)
    route = dest_col.reshape(held) * CELLS + mu_block.reshape(held) * CB + col_block.reshape(held)
    outgoing = pack(tiles.reshape(held, rows, cols), route)
    near = lax.all_gather(theirs, "col", axis=0, tiled=True, axis_index_groups=Y_GROUPS)
    outgoing, own, near = lax.optimization_barrier((outgoing, own, near))
    arrived = lax.all_to_all(outgoing, "col", split_axis=0, concat_axis=0, tiled=True)

    own = own.reshape(NY, WIDE, mu_rows)[:, :per].reshape(NY * per, mu_rows)
    own = lax.all_gather(own, "col", axis=0, tiled=True, axis_index_groups=X_GROUPS)
    left = lax.ppermute(near, "col", x_shift(1))
    right = lax.ppermute(near, "col", x_shift(-1))
    cut = near.shape[0] // 2
    far0 = lax.ppermute(left[:cut], "col", x_shift(1))
    far1 = lax.ppermute(right[cut:], "col", x_shift(-1))

    labels = arrived[:, CAP * rows, :CAP].astype(jnp.int32)
    dense = place(labels, arrived, mu_rows)
    keep, send = contract(where, own, near, left, right, far0, far1, dense)
    share = keep + lax.ppermute(send, "row", CORE_SWAP)
    share = lax.all_to_all(
        share.reshape(NEAR, 2 * OUT_ROWS, -1), "row", split_axis=0, concat_axis=0, tiled=True, axis_index_groups=NEAR_GROUPS
    )
    away = jnp.sum(share[:, OUT_ROWS:], axis=0)
    result = jnp.sum(share[:, :OUT_ROWS], axis=0) + lax.ppermute(away, "row", FAR_SWAP)
    return result.astype(jnp.bfloat16)


def solution(mesh):
    in_specs = (
        P("row", "col", None, None, None),
        P("row", "col", None, None),
        P("row", "col", None),
        P("row", "col", None),
        P("row", "col"),
    )
    return jax.shard_map(per_device, mesh=mesh, in_specs=in_specs, out_specs=P("row", "col"), check_vma=False)
```

```python
import jax
import jax.numpy as jnp
from jax import lax
from jax.experimental import pallas as pl
from jax.experimental.pallas import tpu as pltpu
from jax.sharding import PartitionSpec as P

CB = 4
CAP = 2
NX, NZH, NY = 4, 2, 8
NZL, NCORE = 6, 2
NEAR = NZL // 2
N_COL = NX * NZH * NY
LABEL_ROWS = 8
TILE_ROWS = 16
CELLS = 128
GROUP = 8
OUT_ROWS = 128
WIDE = 32


def device(zl, core, x, zh, y):
    return (((zl * NCORE + core) * NX + x) * NZH + zh) * NY + y


def column(x, zh, y):
    return (x * NZH + zh) * NY + y


X_GROUPS = [[column(x, zh, y) for x in range(NX)] for zh in range(NZH) for y in range(NY)]
Y_GROUPS = [[column(x, zh, y) for y in range(NY)] for x in range(NX) for zh in range(NZH)]
NEAR_GROUPS = [
    [zl * NCORE + core for zl in range(half * NEAR, (half + 1) * NEAR)]
    for half in range(NZL // NEAR)
    for core in range(NCORE)
]
FAR_SWAP = [
    (zl * NCORE + core, (zl + NEAR) % NZL * NCORE + core) for zl in range(NZL) for core in range(NCORE)
]
PLANE_SWAP = [
    (column(x, zh, y), column(x, 1 - zh, y)) for x in range(NX) for zh in range(NZH) for y in range(NY)
]
CORE_SWAP = [(zl * NCORE + core, zl * NCORE + 1 - core) for zl in range(NZL) for core in range(NCORE)]


def x_shift(by):
    return [
        (column(x, zh, y), column((x + by) % NX, zh, y))
        for x in range(NX)
        for zh in range(NZH)
        for y in range(NY)
    ]


def pack_kernel(route, tiles, out, labels, count):
    held, rows, cols = tiles.shape

    @pl.loop(0, N_COL)
    def _(c):
        count[c] = 0
        labels[c] = jnp.zeros((TILE_ROWS, cols), labels.dtype)

    lane = lax.broadcasted_iota(jnp.int32, (TILE_ROWS, cols), 1)

    @pl.loop(0, held)
    def _(t):
        c = route[t] // CELLS
        slot = count[c]
        count[c] = slot + 1
        out[c, pl.ds(pl.multiple_of(slot * rows, rows), rows), :] = tiles[t]
        label = (route[t] % CELLS + 1).astype(jnp.float32)
        labels[c] = jnp.where(lane == slot, label, labels[c].astype(jnp.float32)).astype(labels.dtype)


SMEM = pl.BlockSpec(memory_space=pltpu.SMEM)
VMEM = pl.BlockSpec(memory_space=pltpu.VMEM)
ANY = pl.BlockSpec(memory_space=pl.ANY)


def pack(tiles, route):
    held, rows, cols = tiles.shape
    out, labels = pl.pallas_call(
        pack_kernel,
        out_shape=(
            jax.ShapeDtypeStruct((N_COL, CAP * rows + LABEL_ROWS, cols), tiles.dtype),
            jax.ShapeDtypeStruct((N_COL, TILE_ROWS, cols), tiles.dtype),
        ),
        in_specs=[SMEM, VMEM],
        out_specs=(VMEM, VMEM),
        scratch_shapes=[pltpu.SMEM((N_COL,), jnp.int32)],
        compiler_params=pltpu.CompilerParams(vmem_limit_bytes=24 << 20),
        cost_estimate=pl.CostEstimate(flops=0, bytes_accessed=4 << 20, transcendentals=0),
        name="pack",
    )(route, tiles)
    return out.at[:, CAP * rows :].set(labels[:, :LABEL_ROWS])


def place_kernel(labels, arrived, dense):
    rows = (arrived.shape[1] - LABEL_ROWS) // CAP
    cols = arrived.shape[2]

    @pl.loop(0, dense.shape[0] // rows)
    def _(m):
        dense[pl.ds(pl.multiple_of(m * rows, rows), rows), :] = jnp.zeros((rows, dense.shape[1]), dense.dtype)

    @pl.loop(0, N_COL)
    def _(j):
        for slot in range(CAP):
            label = labels[j, slot]

            @pl.when(label > 0)
            def _():
                cell = label - 1
                row = pl.multiple_of((cell // CB) * rows, rows)
                col = pl.multiple_of(cell % CB * cols, cols)
                dense[pl.ds(row, rows), pl.ds(col, cols)] = arrived[j, pl.ds(slot * rows, rows), :]


def place(labels, arrived, mu_rows):
    return pl.pallas_call(
        place_kernel,
        out_shape=jax.ShapeDtypeStruct((mu_rows, CB * arrived.shape[2]), arrived.dtype),
        in_specs=[SMEM, VMEM],
        out_specs=VMEM,
        compiler_params=pltpu.CompilerParams(vmem_limit_bytes=24 << 20),
        cost_estimate=pl.CostEstimate(flops=0, bytes_accessed=4 << 20, transcendentals=0),
        name="place",
    )(labels, arrived)


def contract_kernel(where, own, near, left, right, far0, far1, dense, keep, send, a, b, total, loads, stores):
    x, plane, zl, core = where[0], where[1], where[2], where[3]
    step = near.shape[0]
    per = step // NY
    groups = OUT_ROWS // GROUP

    parts = [(0, near), (step, left), (2 * step, right), (3 * step, far0), (3 * step + far0.shape[0], far1)]
    copies = [
        pltpu.make_async_copy(ref, b.at[pl.ds(at, ref.shape[0])], loads.at[n]) for n, (at, ref) in enumerate(parts)
    ]
    copies.append(pltpu.make_async_copy(own, a, loads.at[len(parts)]))
    for copy in copies:
        copy.start()

    def store(c, block):
        for i in range(per // GROUP):
            g = c * (per // GROUP) + i
            away = jnp.where(g // groups % NCORE == core, 0, 1)
            to = g // (groups * NCORE)
            slot = to % NEAR * 2 + jnp.where(to // NEAR == zl // NEAR, 0, 1)
            row = pl.multiple_of((slot * groups + g % groups) * GROUP, GROUP)
            total[away, pl.ds(row, GROUP), :] = block[i * GROUP : (i + 1) * GROUP]

    def multiply(block, columns, side):
        product = jnp.dot(block, dense[...], preferred_element_type=jnp.float32)
        for n, xx in enumerate(columns):
            for y in range(NY):
                row = n * step + y * per
                store((xx * NZH + side) * NY + y, product[row : row + per])

    for copy in copies[:3]:
        copy.wait()
    multiply(b[: 2 * step, :], (x, (x + NX - 1) % NX), 1 - plane)
    for copy in copies[3:5]:
        copy.wait()
    multiply(b[2 * step :, :], ((x + 1) % NX, (x + 2) % NX), 1 - plane)
    copies[5].wait()
    for n in range(0, NX, 2):
        multiply(a[n * step : (n + 2) * step, :], (n, n + 1), plane)
    out = [pltpu.make_async_copy(total.at[k], ref, stores.at[k]) for k, ref in enumerate((keep, send))]
    for copy in out:
        copy.start()
    for copy in out:
        copy.wait()


def contract(where, own, near, left, right, far0, far1, dense):
    occ, (mu_rows, width) = own.shape[0] * NZH, dense.shape
    shape = jax.ShapeDtypeStruct((occ // NCORE, width), jnp.float32)
    return pl.pallas_call(
        contract_kernel,
        out_shape=(shape, shape),
        in_specs=[SMEM] + [ANY] * 6 + [VMEM],
        out_specs=(ANY, ANY),
        scratch_shapes=[
            pltpu.VMEM(own.shape, own.dtype),
            pltpu.VMEM(own.shape, own.dtype),
            pltpu.VMEM((NCORE, *shape.shape), jnp.float32),
            pltpu.SemaphoreType.DMA((6,)),
            pltpu.SemaphoreType.DMA((NCORE,)),
        ],
        compiler_params=pltpu.CompilerParams(vmem_limit_bytes=52 << 20),
        cost_estimate=pl.CostEstimate(flops=2 * occ * mu_rows * width, bytes_accessed=12 << 20, transcendentals=0),
        name="contract",
    )(where, own, near, left, right, far0, far1, dense)


def per_device(tiles, dest_col, mu_block, col_block, coeff):
    held, rows, cols = tiles.shape[2:]
    mu_rows, per = coeff.shape
    here, row = lax.axis_index("col"), lax.axis_index("row")
    where = jnp.stack([here // (NZH * NY), here // NY % NZH, row // NCORE, row % NCORE]).astype(jnp.int32)

    mine = coeff.T
    padded = jnp.pad(mine, ((0, WIDE - per), (0, 0)))
    own = lax.all_gather(padded, "col", axis=0, tiled=True, axis_index_groups=Y_GROUPS)
    theirs = lax.ppermute(mine, "col", PLANE_SWAP)
    route = dest_col.reshape(held) * CELLS + mu_block.reshape(held) * CB + col_block.reshape(held)
    outgoing = pack(tiles.reshape(held, rows, cols), route)
    near = lax.all_gather(theirs, "col", axis=0, tiled=True, axis_index_groups=Y_GROUPS)
    outgoing, own, near = lax.optimization_barrier((outgoing, own, near))
    arrived = lax.all_to_all(outgoing, "col", split_axis=0, concat_axis=0, tiled=True)

    own = own.reshape(NY, WIDE, mu_rows)[:, :per].reshape(NY * per, mu_rows)
    own = lax.all_gather(own, "col", axis=0, tiled=True, axis_index_groups=X_GROUPS)
    left = lax.ppermute(near, "col", x_shift(1))
    right = lax.ppermute(near, "col", x_shift(-1))
    cut = near.shape[0] // 2
    far0 = lax.ppermute(left[:cut], "col", x_shift(1))
    far1 = lax.ppermute(right[cut:], "col", x_shift(-1))

    labels = arrived[:, CAP * rows, :CAP].astype(jnp.int32)
    dense = place(labels, arrived, mu_rows)
    keep, send = contract(where, own, near, left, right, far0, far1, dense)
    share = keep + lax.ppermute(send, "row", CORE_SWAP)
    share = lax.all_to_all(
        share.reshape(NEAR, 2 * OUT_ROWS, -1), "row", split_axis=0, concat_axis=0, tiled=True, axis_index_groups=NEAR_GROUPS
    )
    away = jnp.sum(share[:, OUT_ROWS:], axis=0)
    result = jnp.sum(share[:, :OUT_ROWS], axis=0) + lax.ppermute(away, "row", FAR_SWAP)
    return result.astype(jnp.bfloat16)


def solution(mesh):
    in_specs = (
        P("row", "col", None, None, None),
        P("row", "col", None, None),
        P("row", "col", None),
        P("row", "col", None),
        P("row", "col"),
    )
    return jax.shard_map(per_device, mesh=mesh, in_specs=in_specs, out_specs=P("row", "col"), check_vma=False)
```
